256 devices in a mesh: aux: 8 (over z_hi, core), row: 8 (over z_lo, y), col: 4 (over x).
Axes of the slice: x: 4, y: 4, z: 8 (z_hi: 4, z_lo: 2; z = z_hi * 2 + z_lo), core: 2. Of those that a mesh axis runs over, the one named last changes fastest.
Arguments:
- act_slab: bfloat16 [30, 1024, 4096], P(None, 'row', ('aux', 'col')), may hold values from -2 to 2
- core_slab: bfloat16 [128, 1024, 4096], P(None, 'col', ('aux', 'row')), may hold values from -2 to 2
- rotation: float32 [30, 30], replicated, may hold values from -1 to 1
- core_block: int32 [1], replicated, may hold values from 0 to 31
- core_energy: float32 [128], replicated, may hold values from -30 to -6
- vir_energy: float32 [1024], replicated, may hold values from 0.5 to 8
- act_energy: float32 [30], replicated, may hold values from -3 to 3
- rdm_two: float32 [30, 30, 30, 30], replicated, may hold values from -6 to 6
Outputs:
- amp_one: float32 [1024, 30, 4, 1024], P(('row', 'aux'), None, None, 'col')
- amp_two: float32 [1024, 30, 4, 1024], P(('row', 'aux'), None, None, 'col')
- pair_energy: float32 [2, 4, 1024], P(None, None, ('row', 'aux'))
The draws below stay inside these ranges and needn't reach their ends.
All inputs are finite; a program needn't handle non-finite values.
Results may differ from the reference program's by a relative error of at most 0.0029.
Values may be sent and summed in bfloat16 or wider, within the bound.
A program may use at most 128 MiB of HBM per device.

```python
import math
import jax
import jax.numpy as jnp
from jax import lax

NV = 1024
NAUX = 4096
NACT = 30
CB = 4
NBLK = 32
NCS = 128


def steps_of(key, extent, cuts, least, top_value):
    def one(dim, parts):
        steps = jax.random.uniform(jax.random.fold_in(jax.random.fold_in(key, 6), dim), (parts,), jnp.float32, least / len(cuts), top_value / len(cuts))
        return jnp.repeat(jnp.exp(steps), extent[dim] // parts).reshape((-1,) + (1,) * (len(extent) - dim - 1))

    factor_of = one(*cuts[0])
    for cut in cuts[1:]:
        factor_of = factor_of * one(*cut)
    return factor_of


def scatter_about(stream_key, extent, width, limit, pieces=(), dtype=jnp.bfloat16):
    entries = jax.random.normal(stream_key, extent, jnp.float32) * width
    if len(pieces) > 0:
        entries = steps_of(stream_key, extent, pieces, -0.22, 0.18) * entries
    return jnp.clip(entries, min=-limit, max=limit).astype(dtype)


def setup_inputs(seed: int = 0) -> dict:
    seeds = jax.random.split(jax.random.key(seed), 9)
    act_slab = scatter_about(seeds[0], (NACT, NV, NAUX), (NAUX ** -0.25), 2.0, ((1, 8), (2, 32)))
    core_slab = scatter_about(seeds[1], (NCS, NV, NAUX), (NAUX ** -0.25), 2.0, ((1, 4), (2, 64)))
    rotation = scatter_about(seeds[2], (NACT, NACT), NACT ** -0.5, 1.0, (), jnp.float32)
    core_block = jax.random.randint(seeds[3], (1,), 0, NBLK).astype(jnp.int32)
    core_energy = jnp.clip(jax.random.uniform(seeds[4], (NCS,), jnp.float32, -30.0, -6.0), -30.0, -6.0)
    vir_energy = jnp.clip(jnp.exp(jax.random.uniform(seeds[5], (NV,), jnp.float32, math.log(0.5), math.log(8.0))), 0.5, 8.0)
    act_energy = jnp.clip(jax.random.uniform(seeds[6], (NACT,), jnp.float32, -3.0, 3.0), -3.0, 3.0)
    rdm_two = scatter_about(seeds[7], (NACT, NACT, NACT, NACT), 0.5, 6.0, (), jnp.float32)
    return dict(act_slab=act_slab, core_slab=core_slab, rotation=rotation, core_block=core_block, core_energy=core_energy, vir_energy=vir_energy, act_energy=act_energy, rdm_two=rdm_two)


def reference(act_slab, core_slab, rotation, core_block, core_energy, vir_energy, act_energy, rdm_two):
    hi = lax.Precision.HIGHEST
    half_act = jnp.einsum("st,sap->tap", rotation, act_slab.astype(jnp.float32), precision=hi).astype(jnp.bfloat16)
    first_core = (core_block[0] * CB).astype(jnp.int32)
    core_rows = lax.dynamic_slice_in_dim(core_slab, first_core, CB, 0)
    core_levels = lax.dynamic_slice_in_dim(core_energy, first_core, CB, 0)
    left_side = half_act.astype(jnp.float32).reshape(NACT * NV, NAUX)
    right_side = core_rows.astype(jnp.float32).reshape(CB * NV, NAUX)
    flat_tiles = jnp.dot(left_side, right_side.T, precision=hi)
    tiles = jnp.transpose(flat_tiles.reshape(NACT, NV, CB, NV), (1, 0, 2, 3))
    trace_one = jnp.einsum("uvtv->ut", rdm_two)
    trace_two = jnp.einsum("uvvt->ut", rdm_two)
    denominator = (vir_energy[:, None, None, None] + act_energy[None, :, None, None]
                   - core_levels[None, None, :, None] + vir_energy[None, None, None, :])
    amp_one = -jnp.einsum("ut,atib->auib", trace_one, tiles, precision=hi) / denominator
    amp_two = -jnp.einsum("ut,atib->auib", trace_two, tiles, precision=hi) / denominator
    energy_one = jnp.sum(amp_one * tiles, axis=(1, 3)).T
    energy_two = jnp.sum(amp_two * tiles, axis=(1, 3)).T
    return amp_one, amp_two, jnp.stack([energy_one, energy_two])
```

```python
import functools

import jax
import jax.numpy as jnp
from jax import lax
from jax.experimental import pallas as pl
from jax.experimental.pallas import tpu as pltpu
from jax.sharding import PartitionSpec as P

NBLK = 32
F32 = jnp.float32
BF16 = jnp.bfloat16
HIGH = lax.Precision.HIGHEST
NT = (((1,), (1,)), ((), ()))

ORDER = (
    ("A", 0, 0, 1), ("T", 0),
    ("C", -1, 0, 0), ("C", 1, 0, 0), ("A", -1, 0, 0), ("A", 1, 0, 0),
    ("A", 1, 0, 1), ("A", -1, 0, 1), ("T", 1), ("C", 2, 0, 0), ("T", 2),
    ("A", 0, -1, 0), ("A", 0, 1, 0), ("C", 0, -1, 0), ("C", 0, 1, 0), ("T", 3), ("T", 4),
    ("A", -1, -1, 0), ("A", -1, 1, 0), ("A", 1, -1, 0), ("A", 1, 1, 0),
    ("C", -1, -1, 0), ("C", -1, 1, 0), ("C", 1, -1, 0), ("C", 1, 1, 0),
    ("A", 0, -1, 1), ("A", 0, 1, 1), ("C", 0, -2, 0), ("C", 0, 2, 0), ("G",),
    ("A", -1, -1, 1), ("A", -1, 1, 1), ("C", -1, -2, 0), ("C", -1, 2, 0),
    ("C", 2, -1, 0), ("C", 2, 1, 0), ("A", 0, 2, 0), ("A", 1, -1, 1), ("A", 1, 1, 1),
    ("C", 0, -3, 0), ("C", 0, 3, 0), ("C", 1, -2, 0), ("C", 1, 2, 0), ("A", 1, 2, 0),
    ("M", 0, 0), ("C", 0, 4, 0), ("A", -1, 2, 0), ("A", 0, 2, 1), ("M", 0, 1),
    ("C", 1, -3, 0), ("C", 1, 3, 0), ("C", 2, -2, 0), ("C", 2, 2, 0),
    ("A", 1, 2, 1), ("C", -1, -3, 0), ("C", -1, 3, 0), ("A", -1, 2, 1),
    ("C", -1, 4, 0), ("C", 1, 4, 0), ("C", 2, -3, 0), ("C", 2, 3, 0),
    ("M", 1, 0), ("M", -1, 0), ("C", 2, 4, 0), ("M", 1, 1), ("M", -1, 1),
    ("M", 2, 0), ("M", 2, 1),
)


def kernel(
    act, core, rdm, rot, block, levels, vir, occ,
    one, two, energy,
    abuf, cbuf, acc, rdmv, amp, mix, tr, ebuf,
    send_sem, recv_a, recv_c, recv_h, recv_e, local_sem, out_sem,
):
    nact = act.shape[0]
    sub = abuf.shape[3]
    aux, row, col = lax.axis_index("aux"), lax.axis_index("row"), lax.axis_index("col")
    h, c = aux // 2, aux % 2
    z, y = h * 2 + row // 4, row % 4

    def device(dx=0, dy=0, dz=0, dc=0):
        zz = (z + dz + 8) % 8
        return (
            (zz // 2) * 2 + (c + dc) % 2,
            (zz % 2) * 4 + (y + dy + 4) % 4,
            (col + dx + 4) % 4,
        )

    def act_slot(dx, dh, dc):
        return (col + dx + 4) % 4, ((h + dh + 4) % 4) * 2 + (c + dc) % 2

    def core_slot(dy, dz, dc):
        a, r, _ = device(dy=dy, dz=dz, dc=dc)
        return a, r

    local = [
        pltpu.make_async_copy(rdm, rdmv, local_sem.at[0]),
        pltpu.make_async_copy(
            act.at[:, pl.ds(pl.multiple_of(aux * sub, sub), sub), :], abuf.at[col, aux], local_sem.at[1]
        ),
        pltpu.make_async_copy(core, cbuf.at[aux, row], local_sem.at[2]),
    ]
    for copy in local:
        copy.start()

    partners = [device(dz=2 * dh, dc=dc) for dh in range(4) for dc in range(2) if (dh, dc) != (0, 0)]
    partners += [device(dx=dx) for dx in (1, -1, 2)]
    partners += [device(dy=dy) for dy in (1, -1)]
    partners += [device(dz=dz) for dz in (1, -1)]
    barrier = pltpu.get_barrier_semaphore()
    for partner in partners:
        pl.semaphore_signal(barrier, inc=1, device_id=partner, device_id_type=pl.DeviceIdType.MESH)
    pl.semaphore_wait(barrier, len(partners))

    sends = []

    def send(src, dst, sem, target):
        copy = pltpu.make_async_remote_copy(
            src_ref=src, dst_ref=dst, send_sem=send_sem.at[len(sends)], recv_sem=sem,
            device_id=target, device_id_type=pl.DeviceIdType.MESH,
        )
        copy.start()
        sends.append(copy)

    def arrived(dst, sem):
        pltpu.make_async_remote_copy(
            src_ref=dst, dst_ref=dst, send_sem=send_sem.at[0], recv_sem=sem,
            device_id=device(dc=1), device_id_type=pl.DeviceIdType.MESH,
        ).wait_recv()

    def scatter_act(dh, dc):
        target = device(dz=2 * dh, dc=dc)
        rows = pl.ds(pl.multiple_of(target[0] * sub, sub), sub)
        send(act.at[:, rows, :], abuf.at[col, aux], recv_a.at[col * 8 + aux], target)

    def pass_act(dx, dh, dc, to):
        x, j = act_slot(dx, dh, dc)
        send(abuf.at[x, j], abuf.at[x, j], recv_a.at[x * 8 + j], device(dx=to))

    def pass_core(from_y, from_z, **to):
        a, r = core_slot(from_y, from_z, 0)
        send(cbuf.at[a, r], cbuf.at[a, r], recv_c.at[a * 8 + r], device(**to))

    def half_core(dz, half, to):
        a, r = core_slot(0, dz, 0)
        sem = recv_h.at[0] if half else recv_c.at[a * 8 + r]
        part = cbuf.at[a, r, pl.ds(2 * half, 2)]
        send(part, part, sem, device(dz=to))

    def on_act(dx, dh, dc):
        if dx == 0 and (dh, dc) != (0, 0):
            pass_act(0, dh, dc, 1)
            pass_act(0, dh, dc, -1)
        if dx == -1 and (dh + dc) % 2 == 0:
            pass_act(-1, dh, dc, 1)
        if dx == 1 and (dh + dc) % 2 == 1:
            pass_act(1, dh, dc, -1)
        if (dx, dh, dc) == (0, 1, 0):
            scatter_act(1, 1)
            scatter_act(-1, 1)
        if (dx, dh, dc) == (0, 1, 1):
            scatter_act(2, 0)
        if (dx, dh, dc) == (0, 2, 0):
            scatter_act(2, 1)

    def on_core(dy, dz):
        if dy == 0:
            if -2 <= dz < 0:
                pass_core(0, dz, dz=1)
            if 0 < dz <= 2:
                pass_core(0, dz, dz=-1)
            if dz == -3:
                half_core(dz, 0, 1)
            if dz == 3:
                half_core(dz, 1, -1)
            pass_core(0, dz, dy=1)
            pass_core(0, dz, dy=-1)
        if dy == -1 and dz % 2 == 0:
            pass_core(-1, dz, dy=1)
        if dy == 1 and dz % 2 == 1:
            pass_core(1, dz, dy=-1)
        pass_core(dy, dz, dc=1)

    scatter_act(1, 0)
    scatter_act(-1, 0)
    mine = act.at[:, pl.ds(pl.multiple_of(aux * sub, sub), sub), :]
    for to in (1, -1):
        send(mine, abuf.at[col, aux], recv_a.at[col * 8 + aux], device(dx=to))
    for to in (dict(dz=1), dict(dz=-1), dict(dy=1), dict(dy=-1), dict(dc=1)):
        send(core, cbuf.at[aux, row], recv_c.at[aux * 8 + row], device(**to))
    scatter_act(0, 1)

    def trace_step(u, carry):
        by_lane = jnp.zeros((nact, nact), F32)
        by_row = jnp.zeros((nact, nact), F32)
        lanes = lax.broadcasted_iota(jnp.int32, (nact, nact), 1)
        rows = lax.broadcasted_iota(jnp.int32, (nact, nact), 0)
        for v in range(nact):
            piece = rdmv[u, v]
            by_lane = jnp.where(lanes == v, piece, by_lane)
            by_row = jnp.where(rows == v, piece, by_row)
        first = jnp.sum(by_lane, axis=1, keepdims=True)
        second = jnp.sum(by_row, axis=0, keepdims=True)
        tr[0] = jnp.where(lanes == u, first, tr[0])
        tr[1] = jnp.where(rows == u, second, tr[1])
        return carry

    def build_mix():
        eye = (
            lax.broadcasted_iota(jnp.int32, (nact, nact), 0) == lax.broadcasted_iota(jnp.int32, (nact, nact), 1)
        ).astype(F32)
        spread = (
            lax.broadcasted_iota(jnp.int32, (256, nact), 0) // 8 == lax.broadcasted_iota(jnp.int32, (256, nact), 1)
        ).astype(F32)
        same = (
            lax.broadcasted_iota(jnp.int32, (8 * nact, 256), 0) % 8
            == lax.broadcasted_iota(jnp.int32, (8 * nact, 256), 1) % 8
        )

        def nt(a, b):
            return lax.dot_general(a, b, NT, precision=HIGH, preferred_element_type=F32)

        turn = rot[...]
        for k, small in enumerate((nt(nt(eye, tr[0]), turn), nt(tr[1], turn), nt(eye, turn))):
            tall = jnp.dot(spread[: 8 * nact], small, precision=HIGH, preferred_element_type=F32)
            full = jnp.where(same, nt(tall, spread), 0.0)
            high = full.astype(BF16)
            low = (full - high.astype(F32)).astype(BF16)
            at = pl.ds(k * 8 * nact, 8 * nact)
            mix[at, 0:256] = high
            mix[at, 256:512] = low
            mix[at, 512:768] = high

    done = []

    def product(dh, dc):
        j = ((h + dh + 4) % 4) * 2 + (c + dc) % 2
        left = jnp.concatenate(
            [abuf[x, j].reshape(nact * sub, abuf.shape[4]) for x in range(4)], axis=1
        )
        first = not done
        done.append(j)

        def step(i, carry):
            right = cbuf[j, :, i].reshape(left.shape[1], cbuf.shape[4])
            out = jnp.dot(left, right, preferred_element_type=F32).reshape(acc.shape[1:])
            acc[i] = out if first else acc[i] + out
            return carry

        lax.fori_loop(0, 4, step, 0)

    waited = set()

    def take_core(dy, dz, dc):
        if (dy, dz, dc) in waited or (dy, dz, dc) == (0, 0, 0):
            return
        waited.add((dy, dz, dc))
        a, r = core_slot(dy, dz, dc)
        if (dy, dz, dc) == (0, 4, 0):
            arrived(cbuf.at[a, r, pl.ds(0, 2)], recv_c.at[a * 8 + r])
            arrived(cbuf.at[a, r, pl.ds(2, 2)], recv_h.at[0])
        else:
            arrived(cbuf.at[a, r], recv_c.at[a * 8 + r])

    for event in ORDER:
        kind = event[0]
        if kind == "A":
            x, j = act_slot(*event[1:])
            arrived(abuf.at[x, j], recv_a.at[x * 8 + j])
            on_act(*event[1:])
        elif kind == "C":
            take_core(*event[1:])
            on_core(event[1], event[2])
        elif kind == "T":
            part = event[1]
            if part == 0:
                local[0].wait()
                tr[...] = jnp.zeros_like(tr)
            lax.fori_loop(part * nact // 5, (part + 1) * nact // 5, trace_step, 0)
        elif kind == "G":
            build_mix()
        else:
            _, dh, dc = event
            if not done:
                local[1].wait()
                local[2].wait()
            x, j = act_slot(2, dh, dc)
            arrived(abuf.at[x, j], recv_a.at[x * 8 + j])
            for dz in (2 * dh - 1, 2 * dh, 2 * dh + 1):
                dz = (dz + 3) % 8 - 3
                for dy in (0, 1, -1, 2):
                    take_core(dy, dz, dc)
            product(dh, dc)

    ebuf[col] = jnp.zeros(ebuf.shape[1:], F32)
    lanes = lax.broadcasted_iota(jnp.int32, (8 * nact, 128), 1)
    rows = lax.broadcasted_iota(jnp.int32, (8 * nact, 128), 0)
    vir_row = vir[pl.ds((row * 128 + aux * sub) // 128, 1), :]
    by_occ = jnp.sum(jnp.where(lanes == rows // 8, occ[...], 0.0), axis=1, keepdims=True)
    by_col = jnp.concatenate([vir[pl.ds(2 * col, 1), :], vir[pl.ds(2 * col + 1, 1), :]], axis=1)
    by_row = [
        jnp.sum(jnp.where(lanes == aux * sub + g * 8 + rows % 8, vir_row, 0.0), axis=1, keepdims=True) + by_occ
        for g in range(2)
    ]
    first_core = block[0] * 4
    slots = lax.broadcasted_iota(jnp.int32, (8, 128), 1)

    def finish(i, carry):
        level = levels[first_core + i]
        for g in range(2):
            at = pl.ds(8 * g, 8)
            tile = acc[i, :, at, :].reshape(8 * nact, acc.shape[3])
            high = tile.astype(BF16)
            low = (tile - high.astype(F32)).astype(BF16)
            pad = jnp.zeros((256 - 8 * nact, acc.shape[3]), BF16)
            right = jnp.concatenate([high, pad, high, pad, low, pad], axis=0)
            mixed = jnp.dot(mix[...], right, preferred_element_type=F32)
            scale = -1.0 / ((by_row[g] - level) + by_col)
            turned = mixed[16 * nact :]
            for k in range(2):
                value = mixed[8 * nact * k : 8 * nact * (k + 1)] * scale
                amp[k, i, :, at, :] = value.reshape(nact, 8, acc.shape[3])
                part = jnp.sum((value * turned).reshape(nact, 8, acc.shape[3]), axis=0)
                part = jnp.sum(part, axis=1, keepdims=True)
                ebuf[col, at, :] = ebuf[col, at, :] + jnp.where(slots == k * 4 + i, part, 0.0)
        for k, out in enumerate((one, two)):
            pltpu.make_async_copy(amp.at[k, i], out.at[i], out_sem.at[k, i]).start()
        return carry

    lax.fori_loop(0, 4, finish, 0)
    for dx in (1, -1, 2):
        send(ebuf.at[col], ebuf.at[col], recv_e.at[col], device(dx=dx))
    for dx in (1, -1, 2):
        x = (col + dx + 4) % 4
        arrived(ebuf.at[x], recv_e.at[x])
    total = ((ebuf[0] + ebuf[1]) + ebuf[2]) + ebuf[3]
    energy[...] = total.T[:8]
    for copy in sends:
        copy.wait_send()
    for i in range(4):
        for k, out in enumerate((one, two)):
            pltpu.make_async_copy(amp.at[k, i], out.at[i], out_sem.at[k, i]).wait()


def shards(act_slab, core_slab, rotation, core_block, core_energy, vir_energy, act_energy, rdm_two):
    block_size = core_slab.shape[0] // NBLK
    nact, tile, depth = act_slab.shape
    sub = tile // lax.axis_size("aux")
    cols, core_depth = core_slab.shape[1:]
    core_rows = lax.dynamic_slice_in_dim(core_slab, core_block[0] * block_size, block_size, 0)
    core_rows = jnp.transpose(core_rows, (0, 2, 1))
    any_space = pl.BlockSpec(memory_space=pl.ANY)
    vmem = pl.BlockSpec(memory_space=pltpu.VMEM)
    smem = pl.BlockSpec(memory_space=pltpu.SMEM)
    out = jax.ShapeDtypeStruct((block_size, nact, sub, cols), F32)
    occ = jnp.pad(act_energy, (0, 128 - nact)).reshape(1, 128)
    one, two, energy = pl.pallas_call(
        kernel,
        out_shape=(out, out, jax.ShapeDtypeStruct((2 * block_size, sub), F32)),
        in_specs=[any_space, any_space, any_space, vmem, smem, smem, vmem, vmem],
        out_specs=(any_space, any_space, vmem),
        scratch_shapes=[
            pltpu.VMEM((4, 8, nact, sub, depth), BF16),
            pltpu.VMEM((8, 8, block_size, core_depth, cols), BF16),
            pltpu.VMEM((block_size, nact, sub, cols), F32),
            pltpu.VMEM(rdm_two.shape, F32),
            pltpu.VMEM((2, block_size, nact, sub, cols), F32),
            pltpu.VMEM((3 * 8 * nact, 768), BF16),
            pltpu.VMEM((2, nact, nact), F32),
            pltpu.VMEM((4, sub, 128), F32),
            pltpu.SemaphoreType.DMA((98,)),
            pltpu.SemaphoreType.DMA((32,)),
            pltpu.SemaphoreType.DMA((64,)),
            pltpu.SemaphoreType.DMA((1,)),
            pltpu.SemaphoreType.DMA((4,)),
            pltpu.SemaphoreType.DMA((3,)),
            pltpu.SemaphoreType.DMA((2, 4)),
        ],
        compiler_params=pltpu.CompilerParams(
            collective_id=0, has_side_effects=True, vmem_limit_bytes=56 * 2**20
        ),
    )(act_slab, core_rows, rdm_two, rotation, core_block, core_energy, vir_energy.reshape(8, 128), occ)
    return (
        jnp.transpose(one, (2, 1, 0, 3)),
        jnp.transpose(two, (2, 1, 0, 3)),
        energy.reshape(2, block_size, sub),
    )


def solution(mesh):
    in_specs = (
        P(None, "row", ("aux", "col")),
        P(None, "col", ("aux", "row")),
        P(),
        P(),
        P(),
        P(),
        P(),
        P(),
    )
    out_specs = (
        P(("row", "aux"), None, None, "col"),
        P(("row", "aux"), None, None, "col"),
        P(None, None, ("row", "aux")),
    )
    return jax.shard_map(shards, mesh=mesh, in_specs=in_specs, out_specs=out_specs, check_vma=False)
```

```python
import jax
import jax.numpy as jnp
from jax import lax
from jax.experimental import pallas as pl
from jax.experimental.pallas import tpu as pltpu
from jax.sharding import PartitionSpec as P

NBLK = 32
F32 = jnp.float32
BF16 = jnp.bfloat16
HIGH = lax.Precision.HIGHEST
NT = (((1,), (1,)), ((), ()))

ORDER = (
    ("A", 0, 0, 1), ("A", -1, 0, 0), ("A", 1, 0, 0), ("C", 0, -1, 0), ("C", 0, 1, 0), ("C", -1, 0, 0),
    ("C", 1, 0, 0), ("T", 0), ("T", 1), ("A", -1, 0, 1), ("A", 1, 0, 1), ("T", 2), ("T", 3), ("C", -1, -1, 0),
    ("C", 1, -1, 0), ("T", 4), ("G",), ("A", 0, -1, 0), ("A", 0, 1, 0), ("C", -1, 1, 0), ("C", 1, 1, 0),
    ("C", 0, -2, 0), ("C", 0, 2, 0), ("C", 2, 0, 0), ("C", 2, -1, 0), ("C", 2, 1, 0), ("A", -1, -1, 0),
    ("A", 1, -1, 0), ("M", 0, 0), ("A", 0, -1, 1), ("A", 0, 1, 1), ("M", 0, 1), ("C", -1, -2, 0),
    ("C", 1, -2, 0), ("A", -1, 1, 0), ("A", 1, 1, 0), ("C", 0, -3, 0), ("C", 0, 3, 0), ("C", -1, 2, 0),
    ("C", 1, 2, 0), ("C", 2, -2, 0), ("A", -1, -1, 1), ("A", 1, -1, 1), ("A", -1, 1, 1), ("A", 1, 1, 1),
    ("C", -1, -3, 0), ("C", 1, -3, 0), ("C", 0, 4, 0), ("C", -1, 3, 0), ("C", 1, 3, 0), ("C", 2, 2, 0),
    ("A", 0, 2, 0), ("M", "far", 0), ("C", 2, -3, 0), ("M", "far", 1), ("A", 0, 2, 1), ("C", -1, 4, 0),
    ("C", 1, 4, 0), ("A", -1, 2, 0), ("A", 1, 2, 0), ("C", 2, 3, 0), ("M", "near", 0), ("C", 2, 4, 0),
    ("M", "near", 1), ("A", -1, 2, 1), ("A", 1, 2, 1), ("M", 2, 0), ("M", 2, 1),
)

NEEDS = {
    0: ((0,), (0, 1, -1)),
    "far": ((1, -1), (1, -1, 2, -2)),
    "near": ((1, -1), (2, -2, 3, -3)),
    2: ((2,), (3, -3, 4)),
}


def kernel(
    act, slab, rdm, rot, block, levels, vir, occ,
    amp_one, amp_two, energy,
    abuf, cbuf, acc, slabv, core, rdmv, mix, tr, ebuf,
    send_sem, recv_a, recv_a2, recv_c, recv_c2, recv_e, local_sem,
):
    nact = act.shape[0]
    sub = abuf.shape[3]
    aux, row, col = lax.axis_index("aux"), lax.axis_index("row"), lax.axis_index("col")
    h, c = aux // 2, aux % 2
    z, y = h * 2 + row // 4, row % 4

    def device(dx=0, dy=0, dz=0, dc=0):
        zz = (z + dz + 8) % 8
        return (
            (zz // 2) * 2 + (c + dc) % 2,
            (zz % 2) * 4 + (y + dy + 4) % 4,
            (col + dx + 4) % 4,
        )

    def act_slot(dx, dh, dc):
        return (col + dx + 4) % 4, ((h + dh + 4) % 4) * 2 + (c + dc) % 2

    def core_slot(dy, dz, dc):
        a, r, _ = device(dy=dy, dz=dz, dc=dc)
        return a, r

    partners = [device(dz=2 * dh, dc=dc) for dh in range(4) for dc in range(2) if (dh, dc) != (0, 0)]
    partners += [device(dx=dx) for dx in (1, -1, 2)]
    partners += [device(dy=dy) for dy in (1, -1)]
    partners += [device(dz=dz) for dz in (1, -1)]
    barrier = pltpu.get_barrier_semaphore()
    for partner in partners:
        pl.semaphore_signal(barrier, inc=1, device_id=partner, device_id_type=pl.DeviceIdType.MESH)

    mine = act.at[:, pl.ds(pl.multiple_of(aux * sub, sub), sub), :]
    local = [
        pltpu.make_async_copy(slab, slabv, local_sem.at[0]),
        pltpu.make_async_copy(mine, abuf.at[col, aux], local_sem.at[1]),
        pltpu.make_async_copy(rdm, rdmv, local_sem.at[2]),
    ]
    for copy in local:
        copy.start()
    first_core = block[0] * core.shape[0]
    local[0].wait()
    for i in range(core.shape[0]):
        core[i] = slabv[first_core + i]
    pl.semaphore_wait(barrier, len(partners))

    sends = []

    def send(src, dst, sem, target):
        copy = pltpu.make_async_remote_copy(
            src_ref=src, dst_ref=dst, send_sem=send_sem.at[len(sends)], recv_sem=sem,
            device_id=target, device_id_type=pl.DeviceIdType.MESH,
        )
        copy.start()
        sends.append(copy)

    def arrived(dst, sem):
        pltpu.make_async_remote_copy(
            src_ref=dst, dst_ref=dst, send_sem=send_sem.at[0], recv_sem=sem,
            device_id=device(dc=1), device_id_type=pl.DeviceIdType.MESH,
        ).wait_recv()

    def scatter_act(dh, dc):
        target = device(dz=2 * dh, dc=dc)
        rows = pl.ds(pl.multiple_of(target[0] * sub, sub), sub)
        send(act.at[:, rows, :], abuf.at[col, aux], recv_a.at[col * 8 + aux], target)

    def pass_act(dx, dh, dc, to):
        x, j = act_slot(dx, dh, dc)
        send(abuf.at[x, j], abuf.at[x, j], recv_a.at[x * 8 + j], device(dx=to))

    def pass_core(from_y, from_z, **to):
        a, r = core_slot(from_y, from_z, 0)
        send(cbuf.at[a, r], cbuf.at[a, r], recv_c.at[a * 8 + r], device(**to))

    def part_act(dx, dh, dc, half, to):
        x, j = act_slot(dx, dh, dc)
        part = abuf.at[x, j, pl.ds(half * (nact // 2), nact // 2)]
        send(part, part, (recv_a2 if half else recv_a).at[x * 8 + j], device(dx=to))

    def part_core(from_y, from_z, half, **to):
        a, r = core_slot(from_y, from_z, 0)
        part = cbuf.at[a, r, pl.ds(2 * half, 2)]
        send(part, part, (recv_c2 if half else recv_c).at[a * 8 + r], device(**to))

    def on_act(dx, dh, dc):
        if dx == 0:
            pass_act(0, dh, dc, 1)
            pass_act(0, dh, dc, -1)
        if dx == -1:
            part_act(-1, dh, dc, 0, 1)
        if dx == 1:
            part_act(1, dh, dc, 1, -1)

    def on_core(dy, dz):
        if dy == 0:
            if -2 <= dz < 0:
                pass_core(0, dz, dz=1)
            if 0 < dz <= 2:
                pass_core(0, dz, dz=-1)
            if dz == -3:
                part_core(0, dz, 0, dz=1)
            if dz == 3:
                part_core(0, dz, 1, dz=-1)
            pass_core(0, dz, dy=1)
            pass_core(0, dz, dy=-1)
        if dy == -1:
            part_core(-1, dz, 0, dy=1)
        if dy == 1:
            part_core(1, dz, 1, dy=-1)
        pass_core(dy, dz, dc=1)
        if (dy, dz) == (0, 1):
            scatter_act(1, 1)
            scatter_act(-1, 1)
        if (dy, dz) == (0, 2):
            scatter_act(2, 0)
        if (dy, dz) == (0, 3):
            scatter_act(2, 1)

    for to in (dict(dz=1), dict(dz=-1), dict(dy=1), dict(dy=-1), dict(dc=1)):
        send(core, cbuf.at[aux, row], recv_c.at[aux * 8 + row], device(**to))
    scatter_act(1, 0)
    scatter_act(-1, 0)
    for to in (1, -1):
        send(mine, abuf.at[col, aux], recv_a.at[col * 8 + aux], device(dx=to))
    scatter_act(0, 1)
    cbuf[aux, row] = core[...]

    def trace_step(u, carry):
        by_lane = jnp.zeros((nact, nact), F32)
        by_row = jnp.zeros((nact, nact), F32)
        lanes = lax.broadcasted_iota(jnp.int32, (nact, nact), 1)
        rows = lax.broadcasted_iota(jnp.int32, (nact, nact), 0)
        for v in range(nact):
            piece = rdmv[u, v]
            by_lane = jnp.where(lanes == v, piece, by_lane)
            by_row = jnp.where(rows == v, piece, by_row)
        first = jnp.sum(by_lane, axis=1, keepdims=True)
        second = jnp.sum(by_row, axis=0, keepdims=True)
        tr[0] = jnp.where(lanes == u, first, tr[0])
        tr[1] = jnp.where(rows == u, second, tr[1])
        return carry

    def build_mix():
        eye = (
            lax.broadcasted_iota(jnp.int32, (nact, nact), 0) == lax.broadcasted_iota(jnp.int32, (nact, nact), 1)
        ).astype(F32)
        tall_row = lax.broadcasted_iota(jnp.int32, (256, nact), 0)
        tall_lane = lax.broadcasted_iota(jnp.int32, (256, nact), 1)
        by_orbital = (tall_row % 32 == tall_lane).astype(F32)
        spread = (tall_row // 8 == tall_lane).astype(F32)
        same = (
            lax.broadcasted_iota(jnp.int32, (256, 256), 0) // 32
            == lax.broadcasted_iota(jnp.int32, (256, 256), 1) % 8
        )

        def nt(a, b):
            return lax.dot_general(a, b, NT, precision=HIGH, preferred_element_type=F32)

        turn = rot[...]
        for k, small in enumerate((nt(nt(eye, tr[0]), turn), nt(tr[1], turn), nt(eye, turn))):
            tall = jnp.dot(by_orbital, small, precision=HIGH, preferred_element_type=F32)
            full = jnp.where(same, nt(tall, spread), 0.0)
            high = full.astype(BF16)
            low = (full - high.astype(F32)).astype(BF16)
            at = pl.ds(k * 256, 256)
            mix[at, 0:256] = high
            mix[at, 256:512] = low
            mix[at, 512:768] = high

    done = []

    def product(which, dc):
        low = row // 4
        away = {0: 0, 2: 2, "far": 2 * low - 1, "near": 1 - 2 * low}[which]
        j = ((h + away + 4) % 4) * 2 + (c + dc) % 2
        left = jnp.concatenate(
            [abuf[x, j].reshape(nact * sub, abuf.shape[4]) for x in range(4)], axis=1
        )
        first = not done
        done.append(j)

        for i in range(acc.shape[0]):
            right = cbuf[j, :, i].reshape(left.shape[1], cbuf.shape[4])
            out = jnp.dot(left, right, preferred_element_type=F32).reshape(acc.shape[1:])
            acc[i] = out if first else acc[i] + out

    waited = {("A", 0, 0, 0), ("C", 0, 0, 0)}

    def take(kind, *at):
        if (kind, *at) in waited:
            return
        waited.add((kind, *at))
        if kind == "A":
            x, j = act_slot(*at)
            if at[0] == 2:
                half = nact // 2
                arrived(abuf.at[x, j, pl.ds(0, half)], recv_a.at[x * 8 + j])
                arrived(abuf.at[x, j, pl.ds(half, half)], recv_a2.at[x * 8 + j])
            else:
                arrived(abuf.at[x, j], recv_a.at[x * 8 + j])
        else:
            a, r = core_slot(*at)
            if at[2] == 0 and (at[0] == 2 or at[1] == 4 and at[0] == 0):
                arrived(cbuf.at[a, r, pl.ds(0, 2)], recv_c.at[a * 8 + r])
                arrived(cbuf.at[a, r, pl.ds(2, 2)], recv_c2.at[a * 8 + r])
            else:
                arrived(cbuf.at[a, r], recv_c.at[a * 8 + r])

    for event in ORDER:
        kind = event[0]
        if kind == "A":
            take(*event)
            on_act(*event[1:])
        elif kind == "C":
            take(*event)
            on_core(event[1], event[2])
        elif kind == "T":
            part = event[1]
            if part == 0:
                local[2].wait()
                tr[...] = jnp.zeros_like(tr)
            lax.fori_loop(part * nact // 5, (part + 1) * nact // 5, trace_step, 0)
        elif kind == "G":
            build_mix()
        else:
            _, which, dc = event
            if not done:
                local[1].wait()
            for dh in NEEDS[which][0]:
                for dx in (0, 1, -1, 2):
                    take("A", dx, dh, dc)
            for dz in NEEDS[which][1]:
                for dy in (0, 1, -1, 2):
                    take("C", dy, dz, dc)
            product(which, dc)

    ebuf[col] = jnp.zeros(ebuf.shape[1:], F32)
    lanes = lax.broadcasted_iota(jnp.int32, (256, 128), 1)
    rows = lax.broadcasted_iota(jnp.int32, (256, 128), 0)
    vir_row = vir[pl.ds(row, 1), :]
    by_occ = jnp.sum(
        jnp.where(
            lax.broadcasted_iota(jnp.int32, (256, nact), 1)
            == lax.broadcasted_iota(jnp.int32, (256, nact), 0) % 32,
            occ[...],
            0.0,
        ),
        axis=1,
        keepdims=True,
    )
    by_col = jnp.concatenate([vir[pl.ds(2 * col, 1), :], vir[pl.ds(2 * col + 1, 1), :]], axis=1)
    slots = lax.broadcasted_iota(jnp.int32, (8, 128), 1)
    for g in range(2):
        at = pl.ds(8 * g, 8)
        by_row = by_occ + jnp.sum(
            jnp.where(lanes == aux * sub + g * 8 + rows // 32, vir_row, 0.0), axis=1, keepdims=True
        )

        def finish(i):
            tile = acc[i, :, at, :].reshape(8 * nact, acc.shape[3])
            high = tile.astype(BF16)
            low = (tile - high.astype(F32)).astype(BF16)
            pad = jnp.zeros((256 - 8 * nact, acc.shape[3]), BF16)
            right = jnp.concatenate([high, pad, high, pad, low, pad], axis=0)
            mixed = jnp.dot(mix[...], right, preferred_element_type=F32)
            scale = -1.0 / ((by_row - levels[first_core + i]) + by_col)
            turned = mixed[512:]
            for k, amp in enumerate((amp_one, amp_two)):
                value = mixed[256 * k : 256 * (k + 1)] * scale
                for half in range(2):
                    amp[pl.ds(g * 2048 + half * 4 + i, 256, stride=8), :] = value[:, 128 * half : 128 * (half + 1)]
                part = jnp.sum((value * turned).reshape(8, 32, acc.shape[3]), axis=1)
                part = jnp.sum(part, axis=1, keepdims=True)
                ebuf[col, at, :] = ebuf[col, at, :] + jnp.where(slots == k * 4 + i, part, 0.0)

        for i in range(acc.shape[0]):
            finish(i)
    for dx in (1, -1, 2):
        send(ebuf.at[col], ebuf.at[col], recv_e.at[col], device(dx=dx))
    for copy in sends[:-3]:
        copy.wait_send()
    for dx in (1, -1, 2):
        x = (col + dx + 4) % 4
        arrived(ebuf.at[x], recv_e.at[x])
    total = (((ebuf[0] + ebuf[1]) + ebuf[2]) + ebuf[3]).T
    energy[0] = total[:4]
    energy[1] = total[4:8]
    for copy in sends[-3:]:
        copy.wait_send()


def place(amp_one, amp_two, energy, one, two, out, sem):
    sub, nact, _, _ = one.shape
    copies = [pltpu.make_async_copy(energy, out, sem.at[4])]
    for k, (amp, to) in enumerate(((amp_one, one), (amp_two, two))):
        for half in range(2):
            copies.append(
                pltpu.make_async_copy(
                    amp.reshape(sub, 32, 8, 128).at[:, pl.ds(0, nact), pl.ds(4 * half, 4), :],
                    to.at[:, :, :, pl.ds(128 * half, 128)],
                    sem.at[2 * k + half],
                )
            )
    for copy in copies:
        copy.start()
    for copy in copies:
        copy.wait()


def shards(act_slab, core_slab, rotation, core_block, core_energy, vir_energy, act_energy, rdm_two):
    block_size = core_slab.shape[0] // NBLK
    nact, tile, depth = act_slab.shape
    sub = tile // lax.axis_size("aux")
    cols, core_depth = core_slab.shape[1:]
    slab = jnp.transpose(core_slab, (0, 2, 1))
    hbm = pl.BlockSpec(memory_space=pltpu.HBM)
    vmem = pl.BlockSpec(memory_space=pltpu.VMEM)
    smem = pl.BlockSpec(memory_space=pltpu.SMEM)
    mixed = pltpu.VMEM((sub * 32 * 2 * block_size, 128), F32)
    parts = pltpu.VMEM((2, block_size, sub), F32)
    amp_one, amp_two, energy = pl.pallas_call(
        kernel,
        out_shape=(mixed, mixed, parts),
        in_specs=[hbm, hbm, hbm, vmem, smem, smem, vmem, vmem],
        out_specs=(vmem, vmem, vmem),
        scratch_shapes=[
            pltpu.VMEM((4, 8, nact, sub, depth), BF16),
            pltpu.VMEM((8, 8, block_size, core_depth, cols), BF16),
            pltpu.VMEM((block_size, nact, sub, cols), F32),
            pltpu.VMEM(slab.shape, BF16),
            pltpu.VMEM((block_size, core_depth, cols), BF16),
            pltpu.VMEM(rdm_two.shape, F32),
            pltpu.VMEM((768, 768), BF16),
            pltpu.VMEM((2, nact, nact), F32),
            pltpu.VMEM((4, sub, 128), F32),
            pltpu.SemaphoreType.DMA((114,)),
            pltpu.SemaphoreType.DMA((32,)),
            pltpu.SemaphoreType.DMA((32,)),
            pltpu.SemaphoreType.DMA((64,)),
            pltpu.SemaphoreType.DMA((64,)),
            pltpu.SemaphoreType.DMA((4,)),
            pltpu.SemaphoreType.DMA((3,)),
        ],
        compiler_params=pltpu.CompilerParams(
            collective_id=0, has_side_effects=True, vmem_limit_bytes=56 * 2**20
        ),
    )(
        act_slab, slab, rdm_two, rotation, core_block, core_energy,
        vir_energy.reshape(8, 128), act_energy.reshape(1, nact),
    )
    out = jax.ShapeDtypeStruct((sub, nact, block_size, cols), F32)
    return tuple(
        pl.pallas_call(
            place,
            out_shape=(out, out, jax.ShapeDtypeStruct(parts.shape, F32)),
            in_specs=[vmem, vmem, vmem],
            out_specs=(hbm, hbm, hbm),
            scratch_shapes=[pltpu.SemaphoreType.DMA((5,))],
            compiler_params=pltpu.CompilerParams(vmem_limit_bytes=16 * 2**20),
        )(amp_one, amp_two, energy)
    )


def solution(mesh):
    in_specs = (
        P(None, "row", ("aux", "col")),
        P(None, "col", ("aux", "row")),
        P(),
        P(),
        P(),
        P(),
        P(),
        P(),
    )
    out_specs = (
        P(("row", "aux"), None, None, "col"),
        P(("row", "aux"), None, None, "col"),
        P(None, None, ("row", "aux")),
    )
    return jax.shard_map(shards, mesh=mesh, in_specs=in_specs, out_specs=out_specs, check_vma=False)
```

```python
import jax
import jax.numpy as jnp
from jax import lax
from jax.experimental import pallas as pl
from jax.experimental.pallas import tpu as pltpu
from jax.sharding import PartitionSpec as P

NBLK = 32
F32 = jnp.float32
BF16 = jnp.bfloat16
HIGH = lax.Precision.HIGHEST
NT = (((1,), (1,)), ((), ()))

ORDER = (
    ("A", 0, 0, 1), ("A", -1, 0, 0), ("A", 1, 0, 0), ("C", 0, -1, 0), ("C", 0, 1, 0), ("S", 1, 1),
    ("S", -1, 1), ("C", -1, 0, 0), ("C", 1, 0, 0), ("T", 0), ("T", 1), ("A", -1, 0, 1), ("A", 1, 0, 1),
    ("T", 2), ("T", 3), ("C", -1, -1, 0), ("C", 1, -1, 0), ("T", 4), ("G",), ("A", 0, -1, 0), ("A", 0, 1, 0),
    ("C", -1, 1, 0), ("C", 1, 1, 0), ("C", 0, -2, 0), ("C", 0, 2, 0), ("S", 2, 0), ("C", 2, -1, 0),
    ("C", 2, 0, 0), ("A", -1, -1, 0), ("A", 1, -1, 0), ("C", -1, -2, 0), ("C", 2, 1, 0), ("A", -1, 1, 0),
    ("A", 1, 1, 0), ("M", 0, 0), ("A", 0, -1, 1), ("A", 0, 1, 1), ("M", 0, 1), ("C", -1, 2, 0),
    ("C", 1, -2, 0), ("C", 0, -3, 0), ("C", 0, 3, 0), ("C", 2, -2, 0), ("C", 1, 2, 0), ("S", 2, 1),
    ("A", -1, -1, 1), ("A", 1, -1, 1), ("A", -1, 1, 1), ("C", 2, 2, 0), ("C", 1, -3, 0), ("C", 0, 4, 0),
    ("M", "far", 0), ("A", 1, 1, 1), ("C", -1, -3, 0), ("C", 1, 3, 0), ("A", 0, 2, 0), ("M", "far", 1),
    ("C", -1, 3, 0), ("C", 2, -3, 0), ("A", 0, 2, 1), ("A", -1, 2, 0), ("A", 1, 2, 0), ("C", -1, 4, 0),
    ("C", 1, 4, 0), ("C", 2, 3, 0), ("M", "near", 0), ("A", -1, 2, 1), ("A", 1, 2, 1), ("M", "near", 1),
    ("C", 2, 4, 0), ("M", 2, 0), ("M", 2, 1),
)

FIRST = ((1, 0), (-1, 0), (0, 1))

SIDE = {('C', 1): 1, ('A', 0, 0): 1, ('A', 0, 1): 1, ('A', 1, 1): -1, ('C', 0): 1, ('A', 1, 0): 1, ('C', 4): 1, ('A', -1, 1): 1, ('C', -3): 1, ('C', 2): -1, ('A', -1, 0): -1, ('C', -2): -1, ('C', -1): -1}

NEEDS = {
    0: ((0,), (0, 1, -1)),
    "far": ((1, -1), (1, -1, 2, -2)),
    "near": ((1, -1), (2, -2, 3, -3)),
    2: ((2,), (3, -3, 4)),
}


def kernel(
    act, slab, rdm, rot, block, levels, vir_one, vir, occ,
    amp_one, amp_two, energy,
    abuf, cbuf, acc, slabv, core, rdmv, mix, tr, parts, ebuf,
    send_sem, recv_a, recv_a2, recv_c, recv_c2, recv_e, local_sem,
):
    nact = act.shape[0]
    sub = abuf.shape[3]
    aux, row, col = lax.axis_index("aux"), lax.axis_index("row"), lax.axis_index("col")
    h, c = lax.div(aux, 2), lax.rem(aux, 2)
    z, y = h * 2 + lax.div(row, 4), lax.rem(row, 4)
    column = [lax.rem(col + dx, 4) for dx in range(4)]
    line = [lax.rem(y + dy, 4) for dy in range(4)]
    core_id = [c, 1 - c]
    level_of = [lax.rem(z + dz, 8) for dz in range(8)]
    group = [[lax.div(zz, 2) * 2 + core_id[dc] for dc in range(2)] for zz in level_of]
    layer = [lax.rem(zz, 2) for zz in level_of]
    rows_of = [[low * 4 + line[dy] for dy in range(4)] for low in layer]

    def device(dx=0, dy=0, dz=0, dc=0):
        return group[dz % 8][dc % 2], rows_of[dz % 8][dy % 4], column[dx % 4]

    def act_slot(dx, dh, dc):
        return column[dx % 4], group[2 * dh % 8][dc % 2]

    def core_slot(dy, dz, dc):
        return group[dz % 8][dc % 2], rows_of[dz % 8][dy % 4]

    partners = [device(dz=2 * dh, dc=dc) for dh in range(4) for dc in range(2) if (dh, dc) != (0, 0)]
    partners += [device(dx=dx) for dx in (1, -1, 2)]
    partners += [device(dy=dy) for dy in (1, -1)]
    partners += [device(dz=dz) for dz in (1, -1)]
    barrier = pltpu.get_barrier_semaphore()
    for partner in partners:
        pl.semaphore_signal(barrier, inc=1, device_id=partner, device_id_type=pl.DeviceIdType.MESH)

    mine = act.at[:, pl.ds(pl.multiple_of(aux * sub, sub), sub), :]
    local = [
        pltpu.make_async_copy(slab, slabv, local_sem.at[0]),
        pltpu.make_async_copy(mine, abuf.at[col, aux], local_sem.at[1]),
        pltpu.make_async_copy(rdm, rdmv, local_sem.at[2]),
    ]
    for copy in local:
        copy.start()
    first_core = block[0] * core.shape[0]
    local[0].wait()
    for i in range(core.shape[0]):
        core[i] = slabv[first_core + i]
    pl.semaphore_wait(barrier, len(partners))

    sends = []

    def send(src, dst, sem, target):
        copy = pltpu.make_async_remote_copy(
            src_ref=src, dst_ref=dst, send_sem=send_sem.at[len(sends)], recv_sem=sem,
            device_id=target, device_id_type=pl.DeviceIdType.MESH,
        )
        copy.start()
        sends.append(copy)

    def arrived(dst, sem):
        pltpu.make_async_remote_copy(
            src_ref=dst, dst_ref=dst, send_sem=send_sem.at[0], recv_sem=sem,
            device_id=device(dc=1), device_id_type=pl.DeviceIdType.MESH,
        ).wait_recv()

    def scatter_act(dh, dc):
        target = device(dz=2 * dh, dc=dc)
        rows = pl.ds(pl.multiple_of(target[0] * sub, sub), sub)
        send(act.at[:, rows, :], abuf.at[col, aux], recv_a.at[col * 8 + aux], target)

    def pass_act(dx, dh, dc, to):
        x, j = act_slot(dx, dh, dc)
        send(abuf.at[x, j], abuf.at[x, j], recv_a.at[x * 8 + j], device(dx=to))

    def pass_core(from_y, from_z, **to):
        a, r = core_slot(from_y, from_z, 0)
        send(cbuf.at[a, r], cbuf.at[a, r], recv_c.at[a * 8 + r], device(**to))

    def part_act(dx, dh, dc, half, to):
        x, j = act_slot(dx, dh, dc)
        part = abuf.at[x, j, pl.ds(half * (nact // 2), nact // 2)]
        send(part, part, (recv_a2 if half else recv_a).at[x * 8 + j], device(dx=to))

    def part_core(from_y, from_z, half, **to):
        a, r = core_slot(from_y, from_z, 0)
        part = cbuf.at[a, r, pl.ds(2 * half, 2)]
        send(part, part, (recv_c2 if half else recv_c).at[a * 8 + r], device(**to))

    def on_act(dx, dh, dc):
        if dx == 0:
            pass_act(0, dh, dc, 1)
            pass_act(0, dh, dc, -1)
        side = SIDE.get(("A", dh, dc), 0)
        if side == 0 and abs(dx) == 1:
            part_act(dx, dh, dc, (dx + 1) // 2, -dx)
        if side != 0 and dx == side:
            pass_act(dx, dh, dc, -dx)

    def on_core(dy, dz):
        if dy == 0:
            if -2 <= dz < 0:
                pass_core(0, dz, dz=1)
            if 0 < dz <= 2:
                pass_core(0, dz, dz=-1)
            if dz == -3:
                part_core(0, dz, 0, dz=1)
            if dz == 3:
                part_core(0, dz, 1, dz=-1)
            pass_core(0, dz, dy=1)
            pass_core(0, dz, dy=-1)
        side = SIDE.get(("C", dz), 0)
        if side == 0 and abs(dy) == 1:
            part_core(dy, dz, (dy + 1) // 2, dy=-dy)
        if side != 0 and dy == side:
            pass_core(dy, dz, dy=-dy)
        pass_core(dy, dz, dc=1)

    for to in (dict(dz=1), dict(dz=-1), dict(dy=1), dict(dy=-1), dict(dc=1)):
        send(core, cbuf.at[aux, row], recv_c.at[aux * 8 + row], device(**to))
    for to in (1, -1):
        send(mine, abuf.at[col, aux], recv_a.at[col * 8 + aux], device(dx=to))
    for event in FIRST:
        scatter_act(*event)
    cbuf[aux, row] = core[...]

    def trace_step(u, carry):
        by_lane = jnp.zeros((nact, nact), F32)
        by_row = jnp.zeros((nact, nact), F32)
        lanes = lax.broadcasted_iota(jnp.int32, (nact, nact), 1)
        rows = lax.broadcasted_iota(jnp.int32, (nact, nact), 0)
        for v in range(nact):
            piece = rdmv[u, v]
            by_lane = jnp.where(lanes == v, piece, by_lane)
            by_row = jnp.where(rows == v, piece, by_row)
        first = jnp.sum(by_lane, axis=1, keepdims=True)
        second = jnp.sum(by_row, axis=0, keepdims=True)
        tr[0] = jnp.where(lanes == u, first, tr[0])
        tr[1] = jnp.where(rows == u, second, tr[1])
        return carry

    def build_mix():
        eye = (
            lax.broadcasted_iota(jnp.int32, (nact, nact), 0) == lax.broadcasted_iota(jnp.int32, (nact, nact), 1)
        ).astype(F32)
        padded = (
            lax.broadcasted_iota(jnp.int32, (32, nact), 0) == lax.broadcasted_iota(jnp.int32, (32, nact), 1)
        ).astype(F32)

        def nt(a, b):
            return lax.dot_general(a, b, NT, precision=HIGH, preferred_element_type=F32)

        turn = rot[...]
        for k, small in enumerate((nt(nt(eye, tr[0]), turn), nt(tr[1], turn), nt(eye, turn))):
            tall = jnp.dot(padded, small, precision=HIGH, preferred_element_type=F32)
            full = nt(tall, padded)
            high = full.astype(BF16)
            low = (full - high.astype(F32)).astype(BF16)
            mix[pl.ds(32 * k, 32), :] = jnp.concatenate([high, low, high, jnp.zeros_like(high)], axis=1)

    done = []

    def product(which, dc):
        low = row // 4
        away = {0: 0, 2: 2, "far": 2 * low - 1, "near": 1 - 2 * low}[which]
        j = ((h + away + 4) % 4) * 2 + (c + dc) % 2
        left = jnp.concatenate(
            [abuf[x, j].reshape(nact * sub, abuf.shape[4]) for x in range(4)], axis=1
        )
        first = not done
        done.append(j)

        for i in range(cbuf.shape[2]):
            right = cbuf[j, :, i].reshape(left.shape[1], cbuf.shape[4])
            out = jnp.dot(left, right, preferred_element_type=F32)
            for half in range(2):
                at = (2 * i + half, pl.ds(0, nact * sub))
                part = out[:, 128 * half : 128 * (half + 1)]
                acc[at] = part if first else acc[at] + part

    waited = {("A", 0, 0, 0), ("C", 0, 0, 0)}

    def take(kind, *at):
        if (kind, *at) in waited:
            return
        waited.add((kind, *at))
        if kind == "A":
            x, j = act_slot(*at)
            if at[0] == 2 and ("A", *at[1:]) not in SIDE:
                half = nact // 2
                arrived(abuf.at[x, j, pl.ds(0, half)], recv_a.at[x * 8 + j])
                arrived(abuf.at[x, j, pl.ds(half, half)], recv_a2.at[x * 8 + j])
            else:
                arrived(abuf.at[x, j], recv_a.at[x * 8 + j])
        else:
            a, r = core_slot(*at)
            halved = at[0] == 2 and ("C", at[1]) not in SIDE or at[:2] == (0, 4)
            if at[2] == 0 and halved:
                arrived(cbuf.at[a, r, pl.ds(0, 2)], recv_c.at[a * 8 + r])
                arrived(cbuf.at[a, r, pl.ds(2, 2)], recv_c2.at[a * 8 + r])
            else:
                arrived(cbuf.at[a, r], recv_c.at[a * 8 + r])

    for event in ORDER:
        kind = event[0]
        if kind == "A":
            take(*event)
            on_act(*event[1:])
        elif kind == "C":
            take(*event)
            on_core(event[1], event[2])
        elif kind == "S":
            scatter_act(*event[1:])
        elif kind == "T":
            part = event[1]
            if part == 0:
                local[2].wait()
                tr[...] = jnp.zeros_like(tr)
                rest = pl.ds(nact * sub, (32 - nact) * sub)
                acc[:, rest, :] = jnp.zeros((acc.shape[0], (32 - nact) * sub, 128), F32)
            lax.fori_loop(part * nact // 5, (part + 1) * nact // 5, trace_step, 0)
        elif kind == "G":
            build_mix()
        else:
            _, which, dc = event
            if not done:
                local[1].wait()
            for dh in NEEDS[which][0]:
                for dx in (0, 1, -1, 2):
                    take("A", dx, dh, dc)
            for dz in NEEDS[which][1]:
                for dy in (0, 1, -1, 2):
                    take("C", dy, dz, dc)
            product(which, dc)

    by_occ = jnp.sum(
        jnp.where(
            lax.broadcasted_iota(jnp.int32, (32, nact), 1) == lax.broadcasted_iota(jnp.int32, (32, nact), 0),
            occ[...],
            0.0,
        ),
        axis=1,
        keepdims=True,
    )
    by_both = by_occ + jnp.concatenate([vir[pl.ds(2 * col, 1), :], vir[pl.ds(2 * col + 1, 1), :]], axis=1)
    count = core.shape[0]
    level = [levels[first_core + i] for i in range(count)]
    for a in range(sub):
        tile = jnp.concatenate(
            [acc[n, pl.ds(a, 32, stride=sub), :] for n in range(acc.shape[0])], axis=1
        )
        high = tile.astype(BF16)
        low = (tile - high.astype(F32)).astype(BF16)
        right = jnp.concatenate([high, high, low, jnp.zeros_like(high)], axis=0)
        mixed = jnp.dot(mix[...], right, preferred_element_type=F32)
        own = vir_one[row * 128 + aux * sub + a]
        for i in range(count):
            at = slice(256 * i, 256 * (i + 1))
            scale = -1.0 / (by_both + (own - level[i]))
            turned = mixed[64:96, at]
            for k, amp in enumerate((amp_one, amp_two)):
                value = mixed[32 * k : 32 * (k + 1), at] * scale
                for half in range(2):
                    amp[pl.ds(a * 256 + half * 4 + i, 32, stride=8), :] = value[:, 128 * half : 128 * (half + 1)]
                part = value * turned
                part = (part[:, :128] + part[:, 128:]).reshape(4, 8, 128)
                parts[(k * count + i) * sub + a] = (part[0] + part[1]) + (part[2] + part[3])
    summed = jnp.sum(jnp.sum(parts[...], axis=1), axis=1, keepdims=True)
    here = lax.broadcasted_iota(jnp.int32, (2 * count * sub, 128), 0) % sub
    spot = here == lax.broadcasted_iota(jnp.int32, (2 * count * sub, 128), 1)
    ebuf[col] = jnp.sum(jnp.where(spot, summed, 0.0).reshape(2 * count, sub, 128), axis=1)
    for dx in (1, -1, 2):
        send(ebuf.at[col], ebuf.at[col], recv_e.at[col], device(dx=dx))
    for copy in sends[:-3]:
        copy.wait_send()
    for dx in (1, -1, 2):
        x = (col + dx + 4) % 4
        arrived(ebuf.at[x], recv_e.at[x])
    total = ((ebuf[0] + ebuf[1]) + ebuf[2]) + ebuf[3]
    energy[0] = total[:count, :sub]
    energy[1] = total[count:, :sub]
    for copy in sends[-3:]:
        copy.wait_send()


def place(amp_one, amp_two, energy, one, two, out, sem):
    sub, nact, _, _ = one.shape
    copies = [pltpu.make_async_copy(energy, out, sem.at[4])]
    for k, (amp, to) in enumerate(((amp_one, one), (amp_two, two))):
        for half in range(2):
            copies.append(
                pltpu.make_async_copy(
                    amp.reshape(sub, 32, 8, 128).at[:, pl.ds(0, nact), pl.ds(4 * half, 4), :],
                    to.at[:, :, :, pl.ds(128 * half, 128)],
                    sem.at[2 * k + half],
                )
            )
    for copy in copies:
        copy.start()
    for copy in copies:
        copy.wait()


def shards(act_slab, core_slab, rotation, core_block, core_energy, vir_energy, act_energy, rdm_two):
    block_size = core_slab.shape[0] // NBLK
    nact, tile, depth = act_slab.shape
    sub = tile // lax.axis_size("aux")
    cols, core_depth = core_slab.shape[1:]
    slab = jnp.transpose(core_slab, (0, 2, 1))
    hbm = pl.BlockSpec(memory_space=pltpu.HBM)
    vmem = pl.BlockSpec(memory_space=pltpu.VMEM)
    smem = pl.BlockSpec(memory_space=pltpu.SMEM)
    mixed = pltpu.VMEM((sub * 32 * 2 * block_size, 128), F32)
    parts = pltpu.VMEM((2, block_size, sub), F32)
    amp_one, amp_two, energy = pl.pallas_call(
        kernel,
        out_shape=(mixed, mixed, parts),
        in_specs=[hbm, hbm, hbm, vmem, smem, smem, smem, vmem, vmem],
        out_specs=(vmem, vmem, vmem),
        scratch_shapes=[
            pltpu.VMEM((4, 8, nact, sub, depth), BF16),
            pltpu.VMEM((8, 8, block_size, core_depth, cols), BF16),
            pltpu.VMEM((2 * block_size, 32 * sub, 128), F32),
            pltpu.VMEM(slab.shape, BF16),
            pltpu.VMEM((block_size, core_depth, cols), BF16),
            pltpu.VMEM(rdm_two.shape, F32),
            pltpu.VMEM((96, 128), BF16),
            pltpu.VMEM((2, nact, nact), F32),
            pltpu.VMEM((2 * block_size * sub, 8, 128), F32),
            pltpu.VMEM((4, 2 * block_size, 128), F32),
            pltpu.SemaphoreType.DMA((114,)),
            pltpu.SemaphoreType.DMA((32,)),
            pltpu.SemaphoreType.DMA((32,)),
            pltpu.SemaphoreType.DMA((64,)),
            pltpu.SemaphoreType.DMA((64,)),
            pltpu.SemaphoreType.DMA((4,)),
            pltpu.SemaphoreType.DMA((3,)),
        ],
        compiler_params=pltpu.CompilerParams(
            collective_id=0, has_side_effects=True, vmem_limit_bytes=56 * 2**20
        ),
    )(
        act_slab, slab, rdm_two, rotation, core_block, core_energy,
        vir_energy, vir_energy.reshape(8, 128), act_energy.reshape(1, nact),
    )
    out = jax.ShapeDtypeStruct((sub, nact, block_size, cols), F32)
    return tuple(
        pl.pallas_call(
            place,
            out_shape=(out, out, jax.ShapeDtypeStruct(parts.shape, F32)),
            in_specs=[vmem, vmem, vmem],
            out_specs=(hbm, hbm, hbm),
            scratch_shapes=[pltpu.SemaphoreType.DMA((5,))],
            compiler_params=pltpu.CompilerParams(vmem_limit_bytes=16 * 2**20),
        )(amp_one, amp_two, energy)
    )


def solution(mesh):
    in_specs = (
        P(None, "row", ("aux", "col")),
        P(None, "col", ("aux", "row")),
        P(),
        P(),
        P(),
        P(),
        P(),
        P(),
    )
    out_specs = (
        P(("row", "aux"), None, None, "col"),
        P(("row", "aux"), None, None, "col"),
        P(None, None, ("row", "aux")),
    )
    return jax.shard_map(shards, mesh=mesh, in_specs=in_specs, out_specs=out_specs, check_vma=False)
```

```python
import jax
import jax.numpy as jnp
from jax import lax
from jax.experimental import pallas as pl
from jax.experimental.pallas import tpu as pltpu
from jax.sharding import PartitionSpec as P

NBLK = 32
F32 = jnp.float32
BF16 = jnp.bfloat16
HIGH = lax.Precision.HIGHEST
NT = (((1,), (1,)), ((), ()))

ORDER = (
    ("A", 0, 0, 1), ("A", -1, 0, 0), ("A", 1, 0, 0), ("C", 0, -1, 0), ("C", 0, 1, 0), ("S", 1, 1),
    ("S", -1, 1), ("C", -1, 0, 0), ("C", 1, 0, 0), ("T", 0), ("T", 1), ("A", -1, 0, 1), ("A", 1, 0, 1),
    ("T", 2), ("T", 3), ("C", -1, -1, 0), ("C", 1, -1, 0), ("T", 4), ("G",), ("A", 0, -1, 0), ("A", 0, 1, 0),
    ("C", -1, 1, 0), ("C", 1, 1, 0), ("C", 0, -2, 0), ("C", 0, 2, 0), ("S", 2, 0), ("C", 2, -1, 0),
    ("C", 2, 0, 0), ("A", -1, -1, 0), ("A", 1, -1, 0), ("C", -1, -2, 0), ("C", 2, 1, 0), ("A", -1, 1, 0),
    ("A", 1, 1, 0), ("M", 0, 0), ("A", 0, -1, 1), ("A", 0, 1, 1), ("M", 0, 1), ("C", -1, 2, 0),
    ("C", 1, -2, 0), ("C", 0, -3, 0), ("C", 0, 3, 0), ("C", 2, -2, 0), ("C", 1, 2, 0), ("S", 2, 1),
    ("A", -1, -1, 1), ("A", 1, -1, 1), ("A", -1, 1, 1), ("C", 2, 2, 0), ("C", 1, -3, 0), ("C", 0, 4, 0),
    ("M", "far", 0), ("A", 1, 1, 1), ("C", -1, -3, 0), ("C", 1, 3, 0), ("A", 0, 2, 0), ("M", "far", 1),
    ("C", -1, 3, 0), ("C", 2, -3, 0), ("A", 0, 2, 1), ("A", -1, 2, 0), ("A", 1, 2, 0), ("C", -1, 4, 0),
    ("C", 1, 4, 0), ("C", 2, 3, 0), ("M", "near", 0), ("A", -1, 2, 1), ("A", 1, 2, 1), ("M", "near", 1),
    ("C", 2, 4, 0), ("M", 2, 0), ("M", 2, 1),
)

FIRST = ((1, 0), (-1, 0), (0, 1))

SIDE = {('C', 1): 1, ('A', 0, 0): 1, ('A', 0, 1): 1, ('A', 1, 1): -1, ('C', 0): 1, ('A', 1, 0): 1, ('C', 4): 1, ('A', -1, 1): 1, ('C', -3): 1, ('C', 2): -1, ('A', -1, 0): -1, ('C', -2): -1, ('C', -1): -1}

NEEDS = {
    0: ((0,), (0, 1, -1)),
    "far": ((1, -1), (1, -1, 2, -2)),
    "near": ((1, -1), (2, -2, 3, -3)),
    2: ((2,), (3, -3, 4)),
}


def kernel(
    act, slab, rdm, rot, block, levels, vir_one, vir, occ,
    amp_one, amp_two, energy,
    abuf, cbuf, acc, slabv, core, rdmv, mix, tr, parts, ebuf,
    send_sem, recv_a, recv_a2, recv_c, recv_c2, recv_e, local_sem,
):
    nact = act.shape[0]
    sub = abuf.shape[3]
    aux, row, col = lax.axis_index("aux"), lax.axis_index("row"), lax.axis_index("col")
    h, c = lax.div(aux, 2), lax.rem(aux, 2)
    z, y = h * 2 + lax.div(row, 4), lax.rem(row, 4)
    column = [lax.rem(col + dx, 4) for dx in range(4)]
    line = [lax.rem(y + dy, 4) for dy in range(4)]
    core_id = [c, 1 - c]
    level_of = [lax.rem(z + dz, 8) for dz in range(8)]
    group = [[lax.div(zz, 2) * 2 + core_id[dc] for dc in range(2)] for zz in level_of]
    layer = [lax.rem(zz, 2) for zz in level_of]
    rows_of = [[low * 4 + line[dy] for dy in range(4)] for low in layer]

    def device(dx=0, dy=0, dz=0, dc=0):
        return group[dz % 8][dc % 2], rows_of[dz % 8][dy % 4], column[dx % 4]

    def act_slot(dx, dh, dc):
        return column[dx % 4], group[2 * dh % 8][dc % 2]

    def core_slot(dy, dz, dc):
        return group[dz % 8][dc % 2], rows_of[dz % 8][dy % 4]

    partners = [device(dz=2 * dh, dc=dc) for dh in range(4) for dc in range(2) if (dh, dc) != (0, 0)]
    partners += [device(dx=dx) for dx in (1, -1, 2)]
    partners += [device(dy=dy) for dy in (1, -1)]
    partners += [device(dz=dz) for dz in (1, -1)]
    barrier = pltpu.get_barrier_semaphore()
    for partner in partners:
        pl.semaphore_signal(barrier, inc=1, device_id=partner, device_id_type=pl.DeviceIdType.MESH)

    mine = act.at[:, pl.ds(pl.multiple_of(aux * sub, sub), sub), :]
    local = [
        pltpu.make_async_copy(slab, slabv, local_sem.at[0]),
        pltpu.make_async_copy(mine, abuf.at[col, aux], local_sem.at[1]),
        pltpu.make_async_copy(rdm, rdmv, local_sem.at[2]),
    ]
    for copy in local:
        copy.start()
    first_core = block[0] * core.shape[0]
    local[0].wait()
    for i in range(core.shape[0]):
        core[i] = slabv[first_core + i]
    pl.semaphore_wait(barrier, len(partners))

    sends = []

    def send(src, dst, sem, target):
        copy = pltpu.make_async_remote_copy(
            src_ref=src, dst_ref=dst, send_sem=send_sem.at[len(sends)], recv_sem=sem,
            device_id=target, device_id_type=pl.DeviceIdType.MESH,
        )
        copy.start()
        sends.append(copy)

    def arrived(dst, sem):
        pltpu.make_async_remote_copy(
            src_ref=dst, dst_ref=dst, send_sem=send_sem.at[0], recv_sem=sem,
            device_id=device(dc=1), device_id_type=pl.DeviceIdType.MESH,
        ).wait_recv()

    def scatter_act(dh, dc):
        target = device(dz=2 * dh, dc=dc)
        rows = pl.ds(pl.multiple_of(target[0] * sub, sub), sub)
        send(act.at[:, rows, :], abuf.at[col, aux], recv_a.at[col * 8 + aux], target)

    def pass_act(dx, dh, dc, to):
        x, j = act_slot(dx, dh, dc)
        send(abuf.at[x, j], abuf.at[x, j], recv_a.at[x * 8 + j], device(dx=to))

    def pass_core(from_y, from_z, **to):
        a, r = core_slot(from_y, from_z, 0)
        send(cbuf.at[a, r], cbuf.at[a, r], recv_c.at[a * 8 + r], device(**to))

    def part_act(dx, dh, dc, half, to):
        x, j = act_slot(dx, dh, dc)
        part = abuf.at[x, j, pl.ds(half * (nact // 2), nact // 2)]
        send(part, part, (recv_a2 if half else recv_a).at[x * 8 + j], device(dx=to))

    def part_core(from_y, from_z, half, **to):
        a, r = core_slot(from_y, from_z, 0)
        part = cbuf.at[a, r, pl.ds(2 * half, 2)]
        send(part, part, (recv_c2 if half else recv_c).at[a * 8 + r], device(**to))

    def on_act(dx, dh, dc):
        if dx == 0:
            pass_act(0, dh, dc, 1)
            pass_act(0, dh, dc, -1)
        side = SIDE.get(("A", dh, dc), 0)
        if side == 0 and abs(dx) == 1:
            part_act(dx, dh, dc, (dx + 1) // 2, -dx)
        if side != 0 and dx == side:
            pass_act(dx, dh, dc, -dx)

    def on_core(dy, dz):
        if dy == 0:
            if -2 <= dz < 0:
                pass_core(0, dz, dz=1)
            if 0 < dz <= 2:
                pass_core(0, dz, dz=-1)
            if dz == -3:
                part_core(0, dz, 0, dz=1)
            if dz == 3:
                part_core(0, dz, 1, dz=-1)
            pass_core(0, dz, dy=1)
            pass_core(0, dz, dy=-1)
        side = SIDE.get(("C", dz), 0)
        if side == 0 and abs(dy) == 1:
            part_core(dy, dz, (dy + 1) // 2, dy=-dy)
        if side != 0 and dy == side:
            pass_core(dy, dz, dy=-dy)
        pass_core(dy, dz, dc=1)

    for to in (dict(dz=1), dict(dz=-1), dict(dy=1), dict(dy=-1), dict(dc=1)):
        send(core, cbuf.at[aux, row], recv_c.at[aux * 8 + row], device(**to))
    for to in (1, -1):
        send(mine, abuf.at[col, aux], recv_a.at[col * 8 + aux], device(dx=to))
    for event in FIRST:
        scatter_act(*event)
    cbuf[aux, row] = core[...]

    def trace_step(u, carry):
        by_lane = jnp.zeros((nact, nact), F32)
        by_row = jnp.zeros((nact, nact), F32)
        lanes = lax.broadcasted_iota(jnp.int32, (nact, nact), 1)
        rows = lax.broadcasted_iota(jnp.int32, (nact, nact), 0)
        for v in range(nact):
            piece = rdmv[u, v]
            by_lane = jnp.where(lanes == v, piece, by_lane)
            by_row = jnp.where(rows == v, piece, by_row)
        first = jnp.sum(by_lane, axis=1, keepdims=True)
        second = jnp.sum(by_row, axis=0, keepdims=True)
        tr[0] = jnp.where(lanes == u, first, tr[0])
        tr[1] = jnp.where(rows == u, second, tr[1])
        return carry

    def build_mix():
        eye = (
            lax.broadcasted_iota(jnp.int32, (nact, nact), 0) == lax.broadcasted_iota(jnp.int32, (nact, nact), 1)
        ).astype(F32)
        padded = (
            lax.broadcasted_iota(jnp.int32, (32, nact), 0) == lax.broadcasted_iota(jnp.int32, (32, nact), 1)
        ).astype(F32)

        def nt(a, b):
            return lax.dot_general(a, b, NT, precision=HIGH, preferred_element_type=F32)

        turn = rot[...]
        for k, small in enumerate((nt(nt(eye, tr[0]), turn), nt(tr[1], turn), nt(eye, turn))):
            tall = jnp.dot(padded, small, precision=HIGH, preferred_element_type=F32)
            full = nt(tall, padded)
            high = full.astype(BF16)
            low = (full - high.astype(F32)).astype(BF16)
            mix[pl.ds(32 * k, 32), :] = jnp.concatenate([high, low, high, jnp.zeros_like(high)], axis=1)

    done = []

    def product(which, dc):
        low = row // 4
        away = {0: 0, 2: 2, "far": 2 * low - 1, "near": 1 - 2 * low}[which]
        j = ((h + away + 4) % 4) * 2 + (c + dc) % 2
        left = jnp.concatenate(
            [abuf[x, j].reshape(nact * sub, abuf.shape[4]) for x in range(4)], axis=1
        )
        first = not done
        done.append(j)

        for i in range(cbuf.shape[2]):
            right = cbuf[j, :, i].reshape(left.shape[1], cbuf.shape[4])
            out = jnp.dot(left, right, preferred_element_type=F32)
            for half in range(2):
                at = (2 * i + half, pl.ds(0, nact * sub))
                part = out[:, 128 * half : 128 * (half + 1)]
                acc[at] = part if first else acc[at] + part

    waited = {("A", 0, 0, 0), ("C", 0, 0, 0)}

    def take(kind, *at):
        if (kind, *at) in waited:
            return
        waited.add((kind, *at))
        if kind == "A":
            x, j = act_slot(*at)
            if at[0] == 2 and ("A", *at[1:]) not in SIDE:
                half = nact // 2
                arrived(abuf.at[x, j, pl.ds(0, half)], recv_a.at[x * 8 + j])
                arrived(abuf.at[x, j, pl.ds(half, half)], recv_a2.at[x * 8 + j])
            else:
                arrived(abuf.at[x, j], recv_a.at[x * 8 + j])
        else:
            a, r = core_slot(*at)
            halved = at[0] == 2 and ("C", at[1]) not in SIDE or at[:2] == (0, 4)
            if at[2] == 0 and halved:
                arrived(cbuf.at[a, r, pl.ds(0, 2)], recv_c.at[a * 8 + r])
                arrived(cbuf.at[a, r, pl.ds(2, 2)], recv_c2.at[a * 8 + r])
            else:
                arrived(cbuf.at[a, r], recv_c.at[a * 8 + r])

    for event in ORDER:
        kind = event[0]
        if kind == "A":
            take(*event)
            on_act(*event[1:])
        elif kind == "C":
            take(*event)
            on_core(event[1], event[2])
        elif kind == "S":
            scatter_act(*event[1:])
        elif kind == "T":
            part = event[1]
            if part == 0:
                local[2].wait()
                tr[...] = jnp.zeros_like(tr)
                rest = pl.ds(nact * sub, (32 - nact) * sub)
                acc[:, rest, :] = jnp.zeros((acc.shape[0], (32 - nact) * sub, 128), F32)
            lax.fori_loop(part * nact // 5, (part + 1) * nact // 5, trace_step, 0)
        elif kind == "G":
            build_mix()
        else:
            _, which, dc = event
            if not done:
                local[1].wait()
            for dh in NEEDS[which][0]:
                for dx in (0, 1, -1, 2):
                    take("A", dx, dh, dc)
            for dz in NEEDS[which][1]:
                for dy in (0, 1, -1, 2):
                    take("C", dy, dz, dc)
            product(which, dc)

    by_occ = jnp.sum(
        jnp.where(
            lax.broadcasted_iota(jnp.int32, (32, nact), 1) == lax.broadcasted_iota(jnp.int32, (32, nact), 0),
            occ[...],
            0.0,
        ),
        axis=1,
        keepdims=True,
    )
    by_both = by_occ + jnp.concatenate([vir[pl.ds(2 * col, 1), :], vir[pl.ds(2 * col + 1, 1), :]], axis=1)
    count = core.shape[0]
    level = [levels[first_core + i] for i in range(count)]
    def mixes(a):
        tile = jnp.concatenate(
            [acc[n, pl.ds(a, 32, stride=sub), :] for n in range(acc.shape[0])], axis=1
        )
        high = tile.astype(BF16)
        low = (tile - high.astype(F32)).astype(BF16)
        right = jnp.concatenate([high, high, low, jnp.zeros_like(high)], axis=0)
        return jnp.dot(mix[...], right, preferred_element_type=F32)

    def scales(a, i):
        own = vir_one[row * 128 + aux * sub + a]
        return -1.0 / (by_both + (own - level[i]))

    for a in range(sub):
        mixed = mixes(a)
        for i in range(count):
            at = slice(256 * i, 256 * (i + 1))
            turned = mixed[64:96, at] * scales(a, i)
            for k in range(2):
                part = mixed[32 * k : 32 * (k + 1), at] * turned
                part = (part[:, :128] + part[:, 128:]).reshape(4, 8, 128)
                parts[(k * count + i) * sub + a] = (part[0] + part[1]) + (part[2] + part[3])
    summed = jnp.sum(jnp.sum(parts[...], axis=1), axis=1, keepdims=True)
    here = lax.broadcasted_iota(jnp.int32, (2 * count * sub, 128), 0) % sub
    spot = here == lax.broadcasted_iota(jnp.int32, (2 * count * sub, 128), 1)
    ebuf[col] = jnp.sum(jnp.where(spot, summed, 0.0).reshape(2 * count, sub, 128), axis=1)
    for dx in (1, -1, 2):
        send(ebuf.at[col], ebuf.at[col], recv_e.at[col], device(dx=dx))
    for a in range(sub):
        mixed = mixes(a)
        for i in range(count):
            at = slice(256 * i, 256 * (i + 1))
            scale = scales(a, i)
            for k, amp in enumerate((amp_one, amp_two)):
                value = mixed[32 * k : 32 * (k + 1), at] * scale
                for half in range(2):
                    amp[pl.ds(a * 256 + half * 4 + i, 32, stride=8), :] = value[:, 128 * half : 128 * (half + 1)]
    for copy in sends[:-3]:
        copy.wait_send()
    for dx in (1, -1, 2):
        x = (col + dx + 4) % 4
        arrived(ebuf.at[x], recv_e.at[x])
    total = ((ebuf[0] + ebuf[1]) + ebuf[2]) + ebuf[3]
    energy[0] = total[:count, :sub]
    energy[1] = total[count:, :sub]
    for copy in sends[-3:]:
        copy.wait_send()


def place(amp_one, amp_two, energy, one, two, out, sem):
    sub, nact, _, _ = one.shape
    copies = [pltpu.make_async_copy(energy, out, sem.at[4])]
    for k, (amp, to) in enumerate(((amp_one, one), (amp_two, two))):
        for half in range(2):
            copies.append(
                pltpu.make_async_copy(
                    amp.reshape(sub, 32, 8, 128).at[:, pl.ds(0, nact), pl.ds(4 * half, 4), :],
                    to.at[:, :, :, pl.ds(128 * half, 128)],
                    sem.at[2 * k + half],
                )
            )
    for copy in copies:
        copy.start()
    for copy in copies:
        copy.wait()


def shards(act_slab, core_slab, rotation, core_block, core_energy, vir_energy, act_energy, rdm_two):
    block_size = core_slab.shape[0] // NBLK
    nact, tile, depth = act_slab.shape
    sub = tile // lax.axis_size("aux")
    cols, core_depth = core_slab.shape[1:]
    slab = jnp.transpose(core_slab, (0, 2, 1))
    hbm = pl.BlockSpec(memory_space=pltpu.HBM)
    vmem = pl.BlockSpec(memory_space=pltpu.VMEM)
    smem = pl.BlockSpec(memory_space=pltpu.SMEM)
    mixed = pltpu.VMEM((sub * 32 * 2 * block_size, 128), F32)
    parts = pltpu.VMEM((2, block_size, sub), F32)
    amp_one, amp_two, energy = pl.pallas_call(
        kernel,
        out_shape=(mixed, mixed, parts),
        in_specs=[hbm, hbm, hbm, vmem, smem, smem, smem, vmem, vmem],
        out_specs=(vmem, vmem, vmem),
        scratch_shapes=[
            pltpu.VMEM((4, 8, nact, sub, depth), BF16),
            pltpu.VMEM((8, 8, block_size, core_depth, cols), BF16),
            pltpu.VMEM((2 * block_size, 32 * sub, 128), F32),
            pltpu.VMEM(slab.shape, BF16),
            pltpu.VMEM((block_size, core_depth, cols), BF16),
            pltpu.VMEM(rdm_two.shape, F32),
            pltpu.VMEM((96, 128), BF16),
            pltpu.VMEM((2, nact, nact), F32),
            pltpu.VMEM((2 * block_size * sub, 8, 128), F32),
            pltpu.VMEM((4, 2 * block_size, 128), F32),
            pltpu.SemaphoreType.DMA((114,)),
            pltpu.SemaphoreType.DMA((32,)),
            pltpu.SemaphoreType.DMA((32,)),
            pltpu.SemaphoreType.DMA((64,)),
            pltpu.SemaphoreType.DMA((64,)),
            pltpu.SemaphoreType.DMA((4,)),
            pltpu.SemaphoreType.DMA((3,)),
        ],
        compiler_params=pltpu.CompilerParams(
            collective_id=0, has_side_effects=True, vmem_limit_bytes=56 * 2**20
        ),
    )(
        act_slab, slab, rdm_two, rotation, core_block, core_energy,
        vir_energy, vir_energy.reshape(8, 128), act_energy.reshape(1, nact),
    )
    out = jax.ShapeDtypeStruct((sub, nact, block_size, cols), F32)
    return tuple(
        pl.pallas_call(
            place,
            out_shape=(out, out, jax.ShapeDtypeStruct(parts.shape, F32)),
            in_specs=[vmem, vmem, vmem],
            out_specs=(hbm, hbm, hbm),
            scratch_shapes=[pltpu.SemaphoreType.DMA((5,))],
            compiler_params=pltpu.CompilerParams(vmem_limit_bytes=16 * 2**20),
        )(amp_one, amp_two, energy)
    )


def solution(mesh):
    in_specs = (
        P(None, "row", ("aux", "col")),
        P(None, "col", ("aux", "row")),
        P(),
        P(),
        P(),
        P(),
        P(),
        P(),
    )
    out_specs = (
        P(("row", "aux"), None, None, "col"),
        P(("row", "aux"), None, None, "col"),
        P(None, None, ("row", "aux")),
    )
    return jax.shard_map(shards, mesh=mesh, in_specs=in_specs, out_specs=out_specs, check_vma=False)
```

```python
import jax
import jax.numpy as jnp
from jax import lax
from jax.experimental import pallas as pl
from jax.experimental.pallas import tpu as pltpu
from jax.sharding import PartitionSpec as P

NBLK = 32
F32 = jnp.float32
BF16 = jnp.bfloat16
HIGH = lax.Precision.HIGHEST
NT = (((1,), (1,)), ((), ()))

ORDER = (
    ("A", 0, 0, 1), ("A", -1, 0, 0), ("A", 1, 0, 0), ("C", 0, -1, 0), ("C", 0, 1, 0), ("S", 1, 1),
    ("S", -1, 1), ("C", -1, 0, 0), ("C", 1, 0, 0), ("T", 0), ("T", 1), ("A", -1, 0, 1), ("A", 1, 0, 1),
    ("T", 2), ("T", 3), ("C", -1, -1, 0), ("C", 1, -1, 0), ("T", 4), ("G",), ("A", 0, -1, 0), ("A", 0, 1, 0),
    ("C", -1, 1, 0), ("C", 1, 1, 0), ("C", 0, -2, 0), ("C", 0, 2, 0), ("S", 2, 0), ("C", 2, -1, 0),
    ("C", 2, 0, 0), ("A", -1, -1, 0), ("A", 1, -1, 0), ("C", -1, -2, 0), ("C", 2, 1, 0), ("A", -1, 1, 0),
    ("A", 1, 1, 0), ("M", 0, 0), ("A", 0, -1, 1), ("A", 0, 1, 1), ("M", 0, 1), ("C", -1, 2, 0),
    ("C", 1, -2, 0), ("C", 0, -3, 0), ("C", 0, 3, 0), ("C", 2, -2, 0), ("C", 1, 2, 0), ("S", 2, 1),
    ("A", -1, -1, 1), ("A", 1, -1, 1), ("A", -1, 1, 1), ("C", 2, 2, 0), ("C", 1, -3, 0), ("C", 0, 4, 0),
    ("M", "far", 0), ("A", 1, 1, 1), ("C", -1, -3, 0), ("C", 1, 3, 0), ("A", 0, 2, 0), ("M", "far", 1),
    ("C", -1, 3, 0), ("C", 2, -3, 0), ("A", 0, 2, 1), ("A", -1, 2, 0), ("A", 1, 2, 0), ("C", -1, 4, 0),
    ("C", 1, 4, 0), ("C", 2, 3, 0), ("M", "near", 0), ("A", -1, 2, 1), ("A", 1, 2, 1), ("M", "near", 1),
    ("C", 2, 4, 0), ("M", 2, 0), ("M", 2, 1),
)

FIRST = ((1, 0), (-1, 0), (0, 1))

SIDE = {('C', 1): 1, ('A', 0, 0): 1, ('A', 0, 1): 1, ('A', 1, 1): -1, ('C', 0): 1, ('A', 1, 0): 1, ('C', 4): 1, ('A', -1, 1): 1, ('C', -3): 1, ('C', 2): -1, ('A', -1, 0): -1, ('C', -2): -1, ('C', -1): -1}

NEEDS = {
    0: ((0,), (0, 1, -1)),
    "far": ((1, -1), (1, -1, 2, -2)),
    "near": ((1, -1), (2, -2, 3, -3)),
    2: ((2,), (3, -3, 4)),
}


def kernel(
    act, slab, rdm, rot, block, levels, vir_one, vir, occ,
    amp_one, amp_two, energy,
    abuf, cbuf, acc, slabv, core, rdmv, mix, scales, tr, parts, ebuf,
    send_sem, recv_a, recv_a2, recv_c, recv_c2, recv_e, local_sem,
):
    nact = act.shape[0]
    sub = abuf.shape[3]
    aux, row, col = lax.axis_index("aux"), lax.axis_index("row"), lax.axis_index("col")
    h, c = lax.div(aux, 2), lax.rem(aux, 2)
    z, y = h * 2 + lax.div(row, 4), lax.rem(row, 4)
    column = [lax.rem(col + dx, 4) for dx in range(4)]
    line = [lax.rem(y + dy, 4) for dy in range(4)]
    core_id = [c, 1 - c]
    level_of = [lax.rem(z + dz, 8) for dz in range(8)]
    group = [[lax.div(zz, 2) * 2 + core_id[dc] for dc in range(2)] for zz in level_of]
    layer = [lax.rem(zz, 2) for zz in level_of]
    rows_of = [[low * 4 + line[dy] for dy in range(4)] for low in layer]

    def device(dx=0, dy=0, dz=0, dc=0):
        return group[dz % 8][dc % 2], rows_of[dz % 8][dy % 4], column[dx % 4]

    def act_slot(dx, dh, dc):
        return column[dx % 4], group[2 * dh % 8][dc % 2]

    def core_slot(dy, dz, dc):
        return group[dz % 8][dc % 2], rows_of[dz % 8][dy % 4]

    partners = [device(dz=2 * dh, dc=dc) for dh in range(4) for dc in range(2) if (dh, dc) != (0, 0)]
    partners += [device(dx=dx) for dx in (1, -1, 2)]
    partners += [device(dy=dy) for dy in (1, -1)]
    partners += [device(dz=dz) for dz in (1, -1)]
    barrier = pltpu.get_barrier_semaphore()
    for partner in partners:
        pl.semaphore_signal(barrier, inc=1, device_id=partner, device_id_type=pl.DeviceIdType.MESH)

    mine = act.at[:, pl.ds(pl.multiple_of(aux * sub, sub), sub), :]
    local = [
        pltpu.make_async_copy(slab, slabv, local_sem.at[0]),
        pltpu.make_async_copy(mine, abuf.at[col, aux], local_sem.at[1]),
        pltpu.make_async_copy(rdm, rdmv, local_sem.at[2]),
    ]
    for copy in local:
        copy.start()
    first_core = block[0] * core.shape[0]
    local[0].wait()
    for i in range(core.shape[0]):
        core[i] = slabv[first_core + i]
    pl.semaphore_wait(barrier, len(partners))

    sends = []

    def send(src, dst, sem, target):
        copy = pltpu.make_async_remote_copy(
            src_ref=src, dst_ref=dst, send_sem=send_sem.at[len(sends)], recv_sem=sem,
            device_id=target, device_id_type=pl.DeviceIdType.MESH,
        )
        copy.start()
        sends.append(copy)

    def arrived(dst, sem):
        pltpu.make_async_remote_copy(
            src_ref=dst, dst_ref=dst, send_sem=send_sem.at[0], recv_sem=sem,
            device_id=device(dc=1), device_id_type=pl.DeviceIdType.MESH,
        ).wait_recv()

    def scatter_act(dh, dc):
        target = device(dz=2 * dh, dc=dc)
        rows = pl.ds(pl.multiple_of(target[0] * sub, sub), sub)
        send(act.at[:, rows, :], abuf.at[col, aux], recv_a.at[col * 8 + aux], target)

    def pass_act(dx, dh, dc, to):
        x, j = act_slot(dx, dh, dc)
        send(abuf.at[x, j], abuf.at[x, j], recv_a.at[x * 8 + j], device(dx=to))

    def pass_core(from_y, from_z, **to):
        a, r = core_slot(from_y, from_z, 0)
        send(cbuf.at[a, r], cbuf.at[a, r], recv_c.at[a * 8 + r], device(**to))

    def part_act(dx, dh, dc, half, to):
        x, j = act_slot(dx, dh, dc)
        part = abuf.at[x, j, pl.ds(half * (nact // 2), nact // 2)]
        send(part, part, (recv_a2 if half else recv_a).at[x * 8 + j], device(dx=to))

    def part_core(from_y, from_z, half, **to):
        a, r = core_slot(from_y, from_z, 0)
        part = cbuf.at[a, r, pl.ds(2 * half, 2)]
        send(part, part, (recv_c2 if half else recv_c).at[a * 8 + r], device(**to))

    def on_act(dx, dh, dc):
        if dx == 0:
            pass_act(0, dh, dc, 1)
            pass_act(0, dh, dc, -1)
        side = SIDE.get(("A", dh, dc), 0)
        if side == 0 and abs(dx) == 1:
            part_act(dx, dh, dc, (dx + 1) // 2, -dx)
        if side != 0 and dx == side:
            pass_act(dx, dh, dc, -dx)

    def on_core(dy, dz):
        if dy == 0:
            if -2 <= dz < 0:
                pass_core(0, dz, dz=1)
            if 0 < dz <= 2:
                pass_core(0, dz, dz=-1)
            if dz == -3:
                part_core(0, dz, 0, dz=1)
            if dz == 3:
                part_core(0, dz, 1, dz=-1)
            pass_core(0, dz, dy=1)
            pass_core(0, dz, dy=-1)
        side = SIDE.get(("C", dz), 0)
        if side == 0 and abs(dy) == 1:
            part_core(dy, dz, (dy + 1) // 2, dy=-dy)
        if side != 0 and dy == side:
            pass_core(dy, dz, dy=-dy)
        pass_core(dy, dz, dc=1)

    for to in (dict(dz=1), dict(dz=-1), dict(dy=1), dict(dy=-1), dict(dc=1)):
        send(core, cbuf.at[aux, row], recv_c.at[aux * 8 + row], device(**to))
    for to in (1, -1):
        send(mine, abuf.at[col, aux], recv_a.at[col * 8 + aux], device(dx=to))
    for event in FIRST:
        scatter_act(*event)
    cbuf[aux, row] = core[...]

    def trace_step(u, carry):
        by_lane = jnp.zeros((nact, nact), F32)
        by_row = jnp.zeros((nact, nact), F32)
        lanes = lax.broadcasted_iota(jnp.int32, (nact, nact), 1)
        rows = lax.broadcasted_iota(jnp.int32, (nact, nact), 0)
        for v in range(nact):
            piece = rdmv[u, v]
            by_lane = jnp.where(lanes == v, piece, by_lane)
            by_row = jnp.where(rows == v, piece, by_row)
        first = jnp.sum(by_lane, axis=1, keepdims=True)
        second = jnp.sum(by_row, axis=0, keepdims=True)
        tr[0] = jnp.where(lanes == u, first, tr[0])
        tr[1] = jnp.where(rows == u, second, tr[1])
        return carry

    def build_mix():
        eye = (
            lax.broadcasted_iota(jnp.int32, (nact, nact), 0) == lax.broadcasted_iota(jnp.int32, (nact, nact), 1)
        ).astype(F32)
        padded = (
            lax.broadcasted_iota(jnp.int32, (32, nact), 0) == lax.broadcasted_iota(jnp.int32, (32, nact), 1)
        ).astype(F32)

        def nt(a, b):
            return lax.dot_general(a, b, NT, precision=HIGH, preferred_element_type=F32)

        turn = rot[...]
        for k, small in enumerate((nt(nt(eye, tr[0]), turn), nt(tr[1], turn), nt(eye, turn))):
            tall = jnp.dot(padded, small, precision=HIGH, preferred_element_type=F32)
            full = nt(tall, padded)
            high = full.astype(BF16)
            low = (full - high.astype(F32)).astype(BF16)
            mix[pl.ds(32 * k, 32), :] = jnp.concatenate([high, low, high, jnp.zeros_like(high)], axis=1)

    done = []

    def product(which, dc):
        low = row // 4
        away = {0: 0, 2: 2, "far": 2 * low - 1, "near": 1 - 2 * low}[which]
        j = ((h + away + 4) % 4) * 2 + (c + dc) % 2
        left = jnp.concatenate(
            [abuf[x, j].reshape(nact * sub, abuf.shape[4]) for x in range(4)], axis=1
        )
        first = not done
        done.append(j)

        for i in range(cbuf.shape[2]):
            right = cbuf[j, :, i].reshape(left.shape[1], cbuf.shape[4])
            out = jnp.dot(left, right, preferred_element_type=F32)
            for half in range(2):
                at = (2 * i + half, pl.ds(0, nact * sub))
                part = out[:, 128 * half : 128 * (half + 1)]
                acc[at] = part if first else acc[at] + part

    waited = {("A", 0, 0, 0), ("C", 0, 0, 0)}

    def take(kind, *at):
        if (kind, *at) in waited:
            return
        waited.add((kind, *at))
        if kind == "A":
            x, j = act_slot(*at)
            if at[0] == 2 and ("A", *at[1:]) not in SIDE:
                half = nact // 2
                arrived(abuf.at[x, j, pl.ds(0, half)], recv_a.at[x * 8 + j])
                arrived(abuf.at[x, j, pl.ds(half, half)], recv_a2.at[x * 8 + j])
            else:
                arrived(abuf.at[x, j], recv_a.at[x * 8 + j])
        else:
            a, r = core_slot(*at)
            halved = at[0] == 2 and ("C", at[1]) not in SIDE or at[:2] == (0, 4)
            if at[2] == 0 and halved:
                arrived(cbuf.at[a, r, pl.ds(0, 2)], recv_c.at[a * 8 + r])
                arrived(cbuf.at[a, r, pl.ds(2, 2)], recv_c2.at[a * 8 + r])
            else:
                arrived(cbuf.at[a, r], recv_c.at[a * 8 + r])

    by_occ = jnp.sum(
        jnp.where(
            lax.broadcasted_iota(jnp.int32, (32, nact), 1) == lax.broadcasted_iota(jnp.int32, (32, nact), 0),
            occ[...],
            0.0,
        ),
        axis=1,
        keepdims=True,
    )
    by_both = by_occ + jnp.concatenate([vir[pl.ds(2 * col, 1), :], vir[pl.ds(2 * col + 1, 1), :]], axis=1)
    count = core.shape[0]
    level = [levels[first_core + i] for i in range(count)]

    def store_scales(a, carry):
        own = vir_one[row * 128 + aux * sub + a]
        for i in range(count):
            scales[a, :, 256 * i : 256 * (i + 1)] = -1.0 / (by_both + (own - level[i]))
        return carry

    for event in ORDER:
        kind = event[0]
        if kind == "A":
            take(*event)
            on_act(*event[1:])
        elif kind == "C":
            take(*event)
            on_core(event[1], event[2])
        elif kind == "S":
            scatter_act(*event[1:])
        elif kind == "T":
            part = event[1]
            if part == 0:
                local[2].wait()
                tr[...] = jnp.zeros_like(tr)
                rest = pl.ds(nact * sub, (32 - nact) * sub)
                acc[:, rest, :] = jnp.zeros((acc.shape[0], (32 - nact) * sub, 128), F32)
            lax.fori_loop(part * nact // 5, (part + 1) * nact // 5, trace_step, 0)
        elif kind == "G":
            build_mix()
            lax.fori_loop(0, sub, store_scales, 0)
        else:
            _, which, dc = event
            if not done:
                local[1].wait()
            for dh in NEEDS[which][0]:
                for dx in (0, 1, -1, 2):
                    take("A", dx, dh, dc)
            for dz in NEEDS[which][1]:
                for dy in (0, 1, -1, 2):
                    take("C", dy, dz, dc)
            product(which, dc)

    def mixes(a):
        tile = jnp.concatenate(
            [acc[n, pl.ds(a, 32, stride=sub), :] for n in range(acc.shape[0])], axis=1
        )
        high = tile.astype(BF16)
        low = (tile - high.astype(F32)).astype(BF16)
        right = jnp.concatenate([high, high, low, jnp.zeros_like(high)], axis=0)
        return jnp.dot(mix[...], right, preferred_element_type=F32)

    for a in range(sub):
        mixed = mixes(a)
        for i in range(count):
            at = slice(256 * i, 256 * (i + 1))
            turned = mixed[64:96, at] * scales[a, :, at]
            for k in range(2):
                part = mixed[32 * k : 32 * (k + 1), at] * turned
                part = (part[:, :128] + part[:, 128:]).reshape(4, 8, 128)
                parts[(k * count + i) * sub + a] = (part[0] + part[1]) + (part[2] + part[3])
    summed = jnp.sum(jnp.sum(parts[...], axis=1), axis=1, keepdims=True)
    here = lax.broadcasted_iota(jnp.int32, (2 * count * sub, 128), 0) % sub
    spot = here == lax.broadcasted_iota(jnp.int32, (2 * count * sub, 128), 1)
    ebuf[col] = jnp.sum(jnp.where(spot, summed, 0.0).reshape(2 * count, sub, 128), axis=1)
    for dx in (1, -1, 2):
        send(ebuf.at[col], ebuf.at[col], recv_e.at[col], device(dx=dx))
    for a in range(sub):
        mixed = mixes(a)
        for i in range(count):
            at = slice(256 * i, 256 * (i + 1))
            scale = scales[a, :, at]
            for k, amp in enumerate((amp_one, amp_two)):
                value = mixed[32 * k : 32 * (k + 1), at] * scale
                for half in range(2):
                    amp[pl.ds(a * 256 + half * 4 + i, 32, stride=8), :] = value[:, 128 * half : 128 * (half + 1)]
    for copy in sends[:-3]:
        copy.wait_send()
    for dx in (1, -1, 2):
        x = (col + dx + 4) % 4
        arrived(ebuf.at[x], recv_e.at[x])
    total = ((ebuf[0] + ebuf[1]) + ebuf[2]) + ebuf[3]
    energy[0] = total[:count, :sub]
    energy[1] = total[count:, :sub]
    for copy in sends[-3:]:
        copy.wait_send()


def place(amp_one, amp_two, energy, one, two, out, sem):
    sub, nact, _, _ = one.shape
    copies = [pltpu.make_async_copy(energy, out, sem.at[4])]
    for k, (amp, to) in enumerate(((amp_one, one), (amp_two, two))):
        for half in range(2):
            copies.append(
                pltpu.make_async_copy(
                    amp.reshape(sub, 32, 8, 128).at[:, pl.ds(0, nact), pl.ds(4 * half, 4), :],
                    to.at[:, :, :, pl.ds(128 * half, 128)],
                    sem.at[2 * k + half],
                )
            )
    for copy in copies:
        copy.start()
    for copy in copies:
        copy.wait()


def shards(act_slab, core_slab, rotation, core_block, core_energy, vir_energy, act_energy, rdm_two):
    block_size = core_slab.shape[0] // NBLK
    nact, tile, depth = act_slab.shape
    sub = tile // lax.axis_size("aux")
    cols, core_depth = core_slab.shape[1:]
    slab = jnp.transpose(core_slab, (0, 2, 1))
    hbm = pl.BlockSpec(memory_space=pltpu.HBM)
    vmem = pl.BlockSpec(memory_space=pltpu.VMEM)
    smem = pl.BlockSpec(memory_space=pltpu.SMEM)
    mixed = pltpu.VMEM((sub * 32 * 2 * block_size, 128), F32)
    parts = pltpu.VMEM((2, block_size, sub), F32)
    amp_one, amp_two, energy = pl.pallas_call(
        kernel,
        out_shape=(mixed, mixed, parts),
        in_specs=[hbm, hbm, hbm, vmem, smem, smem, smem, vmem, vmem],
        out_specs=(vmem, vmem, vmem),
        scratch_shapes=[
            pltpu.VMEM((4, 8, nact, sub, depth), BF16),
            pltpu.VMEM((8, 8, block_size, core_depth, cols), BF16),
            pltpu.VMEM((2 * block_size, 32 * sub, 128), F32),
            pltpu.VMEM(slab.shape, BF16),
            pltpu.VMEM((block_size, core_depth, cols), BF16),
            pltpu.VMEM(rdm_two.shape, F32),
            pltpu.VMEM((96, 128), BF16),
            pltpu.VMEM((sub, 32, block_size * cols), F32),
            pltpu.VMEM((2, nact, nact), F32),
            pltpu.VMEM((2 * block_size * sub, 8, 128), F32),
            pltpu.VMEM((4, 2 * block_size, 128), F32),
            pltpu.SemaphoreType.DMA((114,)),
            pltpu.SemaphoreType.DMA((32,)),
            pltpu.SemaphoreType.DMA((32,)),
            pltpu.SemaphoreType.DMA((64,)),
            pltpu.SemaphoreType.DMA((64,)),
            pltpu.SemaphoreType.DMA((4,)),
            pltpu.SemaphoreType.DMA((3,)),
        ],
        compiler_params=pltpu.CompilerParams(
            collective_id=0, has_side_effects=True, vmem_limit_bytes=56 * 2**20
        ),
    )(
        act_slab, slab, rdm_two, rotation, core_block, core_energy,
        vir_energy, vir_energy.reshape(8, 128), act_energy.reshape(1, nact),
    )
    out = jax.ShapeDtypeStruct((sub, nact, block_size, cols), F32)
    return tuple(
        pl.pallas_call(
            place,
            out_shape=(out, out, jax.ShapeDtypeStruct(parts.shape, F32)),
            in_specs=[vmem, vmem, vmem],
            out_specs=(hbm, hbm, hbm),
            scratch_shapes=[pltpu.SemaphoreType.DMA((5,))],
            compiler_params=pltpu.CompilerParams(vmem_limit_bytes=16 * 2**20),
        )(amp_one, amp_two, energy)
    )


def solution(mesh):
    in_specs = (
        P(None, "row", ("aux", "col")),
        P(None, "col", ("aux", "row")),
        P(),
        P(),
        P(),
        P(),
        P(),
        P(),
    )
    out_specs = (
        P(("row", "aux"), None, None, "col"),
        P(("row", "aux"), None, None, "col"),
        P(None, None, ("row", "aux")),
    )
    return jax.shard_map(shards, mesh=mesh, in_specs=in_specs, out_specs=out_specs, check_vma=False)
```
